32 devices in a mesh: fsdp: 8 (over y, x, core), tensor: 4 (over z).
Axes of the slice: x: 2, y: 2, z: 4, core: 2. Of those that a mesh axis runs over, the one named last changes fastest.
Arguments:
- hidden: bfloat16 [2, 8192, 768], P(None, ('fsdp', 'tensor')), may hold values from -6 to 6
- passages: bfloat16 [2, 20480, 768], P(None, ('fsdp', 'tensor')), may hold values from -6 to 6
- block_ids: int32 [2, 8192], P(None, 'fsdp'), may hold values from 0 to 8191, as said below
- buckets: int32 [256, 256], replicated, may hold values from 0 to 31
- norm_gains: bfloat16 [768, 3], P('fsdp'), may hold values from 0.099609375 to 1.8984375
- self_query: bfloat16 [768, 768], P('fsdp', 'tensor'), may hold values from -0.109375 to 0.109375
- self_key: bfloat16 [768, 768], P('fsdp', 'tensor'), may hold values from -0.109375 to 0.109375
- self_value: bfloat16 [768, 768], P('fsdp', 'tensor'), may hold values from -0.21875 to 0.21875
- self_out: bfloat16 [768, 768], P('fsdp', 'tensor'), may hold values from -0.4375 to 0.4375
- cross_query: bfloat16 [768, 768], P('fsdp', 'tensor'), may hold values from -0.109375 to 0.109375
- cross_key: bfloat16 [768, 768], P('fsdp', 'tensor'), may hold values from -0.109375 to 0.109375
- cross_value: bfloat16 [768, 768], P('fsdp', 'tensor'), may hold values from -0.21875 to 0.21875
- cross_out: bfloat16 [768, 768], P('fsdp', 'tensor'), may hold values from -0.4375 to 0.4375
- ffn_in: bfloat16 [768, 3072], P('fsdp', 'tensor'), may hold values from -0.21875 to 0.21875
- ffn_out: bfloat16 [768, 3072], P('fsdp', 'tensor'), may hold values from -0.15625 to 0.15625
- rel_bias: float32 [32, 12], replicated, may hold values from -4 to 4
- out_grad: bfloat16 [2, 8192, 768], P(None, ('fsdp', 'tensor')), may hold values from -6 to 6
Outputs:
- output: bfloat16 [2, 8192, 768], P(None, ('fsdp', 'tensor'))
- hidden_grad: float32 [2, 8192, 768], P(None, ('fsdp', 'tensor'))
- passages_grad: float32 [2, 20480, 768], P(None, ('fsdp', 'tensor'))
- norm_gains_grad: float32 [768, 3], replicated
- self_query_grad: float32 [768, 768], P('fsdp', 'tensor')
- self_key_grad: float32 [768, 768], P('fsdp', 'tensor')
- self_value_grad: float32 [768, 768], P('fsdp', 'tensor')
- self_out_grad: float32 [768, 768], P('fsdp', 'tensor')
- cross_query_grad: float32 [768, 768], P('fsdp', 'tensor')
- cross_key_grad: float32 [768, 768], P('fsdp', 'tensor')
- cross_value_grad: float32 [768, 768], P('fsdp', 'tensor')
- cross_out_grad: float32 [768, 768], P('fsdp', 'tensor')
- ffn_in_grad: float32 [768, 3072], P('fsdp', 'tensor')
- ffn_out_grad: float32 [768, 3072], P('fsdp', 'tensor')
- rel_bias_grad: float32 [32, 12], replicated
The draws below stay inside these ranges and needn't reach their ends.
Inputs may be any that keep to these rules, and one draw needn't show every extreme that they name: `block_ids`: along each row a token's id is 256 times the index of its aligned window plus the position, inside that window, of the first token of its segment; so ids never fall and a segment never crosses aligned windows of 256 tokens.
All inputs are finite; a program needn't handle non-finite values.
Results may differ from the reference program's by a relative error of at most 0.024.
The reference program's roundings to bfloat16 on the way count: a program that leaves them out, or rounds other values in their place, can miss the bound.
Values may be sent and summed in bfloat16 or wider, within the bound.
No kernel may reach another device: no remote copies, remote signals or barrier semaphores. Data moves between devices by JAX's collectives and lax.ppermute only.
A program may use at most 256 MiB of HBM per device.

```python
import jax
import jax.numpy as jnp
from jax import lax

D = 768
H = 12
DH = 64
FF = 3072
NB = 32
WIN = 256
MB = 2
SEQ = 1024
HD = 768
ENC = 2560
TOKENS = 8192
N_FSDP = 8


def draw_block_ids(key, part):
    windows = TOKENS // WIN
    marks = jax.random.randint(key, (MB, windows, WIN), 0, WIN // 4)
    positions = jnp.arange(WIN, dtype=jnp.int32)
    starts = jnp.where((marks == 0) & (positions[None, None, :] > 0), positions[None, None, :], 0).astype(jnp.int32)
    starts = lax.cummax(starts, axis=2)
    window_base = (jnp.arange(windows, dtype=jnp.int32) * WIN)[None, :, None]
    return (window_base + starts).reshape(MB, TOKENS).astype(jnp.int32)


def place_ends(entries, own_key, low, top_value):
    place = [jax.random.randint(jax.random.fold_in(own_key, axis), (), 0, length) for axis, length in enumerate(entries.shape)]
    main_axis = entries.shape.index(max(entries.shape))
    beside = place[:main_axis] + [(place[main_axis] + 1) % entries.shape[main_axis]] + place[main_axis + 1:]
    return entries.at[tuple(place)].set(low).at[tuple(beside)].set(top_value)


def strengthened(entries, rng, source, target, shards_of, factor):
    owner, partner = [(jnp.arange(entries.shape[axis_at]) // (entries.shape[axis_at] // shards_of)).reshape([-1 if axis == axis_at else 1 for axis in range(entries.ndim)]) for axis_at in (source, target)]
    chosen = jax.random.permutation(rng, shards_of)[partner]
    strong = (owner == chosen) | (owner == (partner + shards_of // 2) % shards_of)
    return jnp.where(strong, factor * entries, entries)


def steps_of(stream_key, shape, cuts, least, high):
    def one(position, parts):
        heights = jax.random.uniform(jax.random.fold_in(jax.random.fold_in(stream_key, 6), position), (parts,), jnp.float32, least / len(cuts), high / len(cuts))
        return jnp.repeat(jnp.exp(heights), shape[position] // parts).reshape((-1,) + (1,) * (len(shape) - position - 1))

    level = one(*cuts[0])
    for cut in cuts[1:]:
        level = level * one(*cut)
    return level


def gaussian(stream_key, extent, width, reach, pieces=(), kind=jnp.bfloat16):
    entries = width * jax.random.normal(stream_key, extent, jnp.float32)
    if pieces:
        entries = entries * steps_of(stream_key, extent, pieces, -0.22, 0.18)
    return jnp.clip(entries, -reach, reach).astype(kind)


def noise_with(own_key, extent, spread, most, cuts, heavy, kind=jnp.bfloat16):
    array = spread * jax.random.normal(own_key, extent, jnp.float32)
    if cuts:
        array = array * steps_of(own_key, extent, cuts, -0.22, 0.18)
    return jnp.clip(strengthened(array, jax.random.fold_in(own_key, 3), *heavy), -most, most).astype(kind)


def setup_inputs(seed: int = 0) -> dict:
    splits = jax.random.split(jax.random.key(seed), 18)
    return {
        "hidden": gaussian(splits[0], (MB, TOKENS, D), 1.0, 6.0, ((1, 32),)),
        "passages": gaussian(splits[1], (MB, N_FSDP * ENC, D), 1.0, 6.0, ((1, 32),)),
        "block_ids": draw_block_ids(jax.random.fold_in(splits[17], 71), 0),
        "buckets": place_ends(jax.random.randint(splits[3], (WIN, WIN), 0, NB), jax.random.fold_in(splits[3], 1), 0, NB - 1).astype(jnp.int32),
        "norm_gains": jnp.clip(1.0 + 0.18 * jax.random.normal(splits[4], (D, 3), jnp.float32), 0.099609375, 1.8984375).astype(jnp.bfloat16),
        "self_query": gaussian(splits[5], (D, HD), (4 * D) ** -0.5, 0.109375, ((0, 8), (1, 4))),
        "self_key": gaussian(splits[6], (D, HD), (4 * D) ** -0.5, 0.109375, ((0, 8), (1, 4))),
        "self_value": gaussian(splits[7], (D, HD), D ** -0.5, 0.21875, ((0, 8), (1, 4))),
        "self_out": gaussian(splits[8], (D, HD), (HD // 4) ** -0.5, 0.4375, ((0, 8), (1, 4))),
        "cross_query": gaussian(splits[9], (D, HD), (4 * D) ** -0.5, 0.109375, ((0, 8), (1, 4))),
        "cross_key": gaussian(splits[10], (D, HD), (4 * D) ** -0.5, 0.109375, ((0, 8), (1, 4))),
        "cross_value": gaussian(splits[11], (D, HD), D ** -0.5, 0.21875, ((0, 8), (1, 4))),
        "cross_out": gaussian(splits[12], (D, HD), (HD // 4) ** -0.5, 0.4375, ((0, 8), (1, 4))),
        "ffn_in": gaussian(splits[13], (D, FF), D ** -0.5, 0.21875, ((0, 8), (1, 4))),
        "ffn_out": gaussian(splits[14], (D, FF), (FF // 2) ** -0.5, 0.15625, ((0, 8), (1, 4))),
        "rel_bias": gaussian(splits[15], (NB, H), 1.0, 4.0, (), jnp.float32),
        "out_grad": noise_with(splits[16], (MB, TOKENS, D), 1.0, 6.0, ((1, 32),), (1, 2, 32, 2.75)),
    }


@jax.custom_vjp
def low(v):
    return lax.optimization_barrier(v.astype(jnp.bfloat16)).astype(jnp.float32)

@jax.custom_vjp
def low_back(v):
    return v

def low_keep(v):
    return (low(v), None)

def low_pass(kept, grad):
    return (grad,)

def back_keep(v):
    return (v, None)

def back_low(kept, grad):
    return (low(grad),)
low.defvjp(low_keep, low_pass)
low_back.defvjp(back_keep, back_low)
EPSILON = 1e-06
MASKED = -1000000000.0
HIGHEST = lax.Precision.HIGHEST

def normalize(stream, gain):
    scale = lax.rsqrt(lax.optimization_barrier(jnp.mean(stream * stream, axis=-1, keepdims=True)) + EPSILON)
    return low(stream * scale * gain)

def project(left, weight):
    return jnp.dot(left, weight, precision=HIGHEST)

def project_back(left, weight):
    return jnp.dot(left, weight.T, precision=HIGHEST)

def split_heads(matrix):
    return matrix.reshape(matrix.shape[0], H, DH)

def attend(scores, value_rows):
    probability = jax.nn.softmax(scores, axis=-1)
    return jnp.einsum('hqk,khd->qhd', low(probability), value_rows, precision=HIGHEST)

def decoder_layer(stream, encoded, segment_ids, buckets, params):
    norm_gains, self_query, self_key, self_value, self_out, cross_query, cross_key, cross_value, cross_out, ffn_in, ffn_out, rel_bias = params
    tile_rows = 2 * WIN if SEQ % (2 * WIN) == 0 else WIN
    tile_count = SEQ // tile_rows
    tile_shape = (tile_count, tile_rows, H, DH)
    normed = normalize(stream, norm_gains[:, 0])
    queries = split_heads(low(low_back(project(normed, self_query))))
    key_rows = split_heads(low(low_back(project(normed, self_key))))
    value_rows = split_heads(low(low_back(project(normed, self_value))))
    window_bias = jnp.transpose(rel_bias[buckets], (2, 0, 1))
    tile_bias = jnp.tile(window_bias, (1, tile_rows // WIN, tile_rows // WIN))
    positions = jnp.arange(tile_rows, dtype=jnp.int32)
    causal = positions[None, :] <= positions[:, None]

    def self_block(inputs_now):
        query_tile, key_tile, value_tile, segment_tile = inputs_now
        raw_scores = jnp.einsum('qhd,khd->hqk', query_tile, key_tile, precision=HIGHEST) + tile_bias
        allowed = (segment_tile[:, None] == segment_tile[None, :]) & causal
        kept = low_back(raw_scores)
        return attend(jnp.where(allowed[None], kept, jnp.full_like(kept, MASKED)), value_tile)
    context = lax.map(jax.checkpoint(self_block), (queries.reshape(tile_shape), key_rows.reshape(tile_shape), value_rows.reshape(tile_shape), segment_ids.reshape(tile_count, tile_rows).astype(jnp.int32)))
    context = low(low_back(context.reshape(SEQ, HD)))
    after_self = stream + low_back(project_back(context, self_out))
    normed_two = normalize(after_self, norm_gains[:, 1])
    cross_rows = split_heads(low(low_back(project(normed_two, cross_query))))
    enc_keys = split_heads(low(low_back(project(encoded, cross_key))))
    enc_values = split_heads(low(low_back(project(encoded, cross_value))))

    def cross_block(query_tile):
        raw_scores = jnp.einsum('qhd,khd->hqk', query_tile, enc_keys, precision=HIGHEST)
        return attend(low_back(raw_scores), enc_values)
    cross_context = lax.map(jax.checkpoint(cross_block), cross_rows.reshape(tile_shape))
    cross_context = low(low_back(cross_context.reshape(SEQ, HD)))
    after_cross = after_self + low_back(project_back(cross_context, cross_out))
    normed_three = normalize(after_cross, norm_gains[:, 2])
    activated = low(jax.nn.gelu(low_back(project(normed_three, ffn_in)), approximate=True))
    return after_cross + low_back(project_back(activated, ffn_out))

def reference(hidden, passages, block_ids, buckets, norm_gains, self_query, self_key, self_value, self_out, cross_query, cross_key, cross_value, cross_out, ffn_in, ffn_out, rel_bias, out_grad):
    sequences = MB * N_FSDP
    params = tuple((weight.astype(jnp.float32) for weight in (norm_gains, self_query, self_key, self_value, self_out, cross_query, cross_key, cross_value, cross_out, ffn_in, ffn_out, rel_bias)))
    streams = hidden.astype(jnp.float32).reshape(sequences, SEQ, D)
    encodings = passages.astype(jnp.float32).reshape(sequences, ENC, D)
    segments = block_ids.astype(jnp.int32).reshape(sequences, SEQ)
    cotangents = out_grad.astype(jnp.float32).reshape(sequences, SEQ, D)
    bucket_table = buckets.astype(jnp.int32)

    def advance(totals, inputs_now):
        stream, encoded, segment_ids, cotangent = inputs_now

        def forward(stream_in, encoded_in, params_in):
            return decoder_layer(stream_in, encoded_in, segment_ids, bucket_table, params_in)
        output, pullback = jax.vjp(forward, stream, encoded, params)
        stream_grad, encoded_grad, param_grads = pullback(cotangent)
        return (jax.tree.map(jnp.add, totals, param_grads), (output.astype(jnp.bfloat16), stream_grad, encoded_grad))
    zero_totals = tuple((jnp.zeros(weight.shape, jnp.float32) for weight in params))
    totals, (outputs, stream_grads, encoded_grads) = lax.scan(advance, zero_totals, (streams, encodings, segments, cotangents))
    return (outputs.reshape(MB, TOKENS, D), stream_grads.reshape(MB, TOKENS, D), encoded_grads.reshape(MB, N_FSDP * ENC, D), totals[0], totals[1], totals[2], totals[3], totals[4], totals[5], totals[6], totals[7], totals[8], totals[9], totals[10], totals[11])
```

```python
import functools

import jax
import jax.numpy as jnp
from jax import lax
from jax.experimental import pallas as pl
from jax.experimental.pallas import tpu as pltpu
from jax.sharding import PartitionSpec as P

DH = 64
WIN = 256
EPSILON = 1e-06
MASKED = -1000000000.0
BF = jnp.bfloat16
F32 = jnp.float32
MIB = 1024 * 1024


def nn(left, right):
    return jnp.dot(left, right, preferred_element_type=F32)


def nt(left, right):
    return lax.dot_general(left, right, (((1,), (1,)), ((), ())), preferred_element_type=F32)


def tn(left, right):
    return lax.dot_general(left, right, (((0,), (0,)), ((), ())), preferred_element_type=F32)


def shift(x, axis, by):
    size = lax.axis_size(axis)
    if by % size == 0:
        return x
    return lax.ppermute(x, axis, [(i, (i + by) % size) for i in range(size)])


def flip(x, axis, bits):
    size = lax.axis_size(axis)
    return lax.ppermute(x, axis, [(i, i ^ bits) for i in range(size)])


def two_way(x, swapped):
    first, second = (4, 2) if swapped else (2, 4)
    return lax.ppermute(x, "fsdp", [(i, i ^ (second if i & 1 else first)) for i in range(8)])


def assemble_kernel(*refs):
    pieces, out_ref = refs[:8], refs[8]
    me = lax.axis_index("fsdp")
    odd = lax.rem(me, 2)
    x_bit, y_bit = lax.rem(me // 2, 2), me // 4

    def flipped(dx, dy, dc):
        new_x = x_bit + dx - 2 * x_bit * dx
        new_y = y_bit + dy - 2 * y_bit * dy
        new_c = odd + dc - 2 * odd * dc
        return new_y * 4 + new_x * 2 + new_c

    even = 1 - odd
    places = [
        flipped(0, 0, 0),
        flipped(even, odd, 0),
        flipped(odd, even, 0),
        flipped(1, 1, 0),
        flipped(0, 0, 1),
        flipped(odd, even, 1),
        flipped(even, odd, 1),
        flipped(1, 1, 1),
    ]
    rows = pieces[0].shape[0]
    for place, piece in zip(places, pieces):
        out_ref[pl.ds(pl.multiple_of(place * rows, rows), rows), :] = piece[...]


def gather_fsdp(piece, widths):
    size = lax.axis_size("fsdp")
    if size != 8 or piece.shape[0] % 16:
        whole = lax.all_gather(piece, "fsdp", axis=0, tiled=True)
        parts, first = [], 0
        for width in widths:
            parts.append(whole[:, first : first + width])
            first += width
        return parts
    one = two_way(piece, False)
    two = two_way(piece, True)
    three = two_way(one, True)
    pieces = [piece, one, two, three]
    pieces = pieces + [flip(p, "fsdp", 1) for p in pieces]
    rows = piece.shape[0]
    parts, first = [], 0
    for width in widths:
        block = 768 if width % 768 == 0 else width
        parts.append(
            pl.pallas_call(
                assemble_kernel,
                grid=(width // block,),
                out_shape=jax.ShapeDtypeStruct((size * rows, width), piece.dtype),
                in_specs=[
                    pl.BlockSpec((rows, block), lambda i, k=first // block: (0, k + i))
                ]
                * 8,
                out_specs=pl.BlockSpec((size * rows, block), lambda i: (0, i)),
                cost_estimate=pl.CostEstimate(
                    flops=0, bytes_accessed=32 * rows * width, transcendentals=0
                ),
            )(*pieces)
        )
        first += width
    return parts


def gather_weights(shards, widths, grouped):
    ranks = lax.axis_size("tensor")
    joined = jnp.concatenate(shards, axis=1)
    blocks = [shift(joined, "tensor", s) for s in range(ranks)]
    if grouped:
        piece = jnp.concatenate(blocks, axis=1)
    else:
        parts, first = [], 0
        for shard in shards:
            parts += [b[:, first : first + shard.shape[1]] for b in blocks]
            first += shard.shape[1]
        piece = jnp.concatenate(parts, axis=1)
    return gather_fsdp(piece, widths)


def gather_small(shard):
    size = lax.axis_size("fsdp")
    held = shard[None]
    bit = 1
    while bit < size:
        held = jnp.concatenate([held, flip(held, "fsdp", bit)], axis=0)
        bit *= 2
    order = jnp.bitwise_xor(jnp.arange(size, dtype=jnp.int32), lax.axis_index("fsdp"))
    return jnp.take(held, order, axis=0)


def sum_everywhere(x):
    for axis in ("fsdp", "tensor"):
        bit = 1
        while bit < lax.axis_size(axis):
            x = x + flip(x, axis, bit)
            bit *= 2
    return x


def pick(x, index):
    return lax.dynamic_index_in_dim(x, index, 0, keepdims=False)


def scatter_fsdp(grad):
    size = lax.axis_size("fsdp")
    if size != 8:
        return lax.psum_scatter(grad.astype(F32), "fsdp", scatter_dimension=0, tiled=True)
    me = lax.axis_index("fsdp")
    odd, chip = lax.rem(me, 2), me // 2
    near = 1 + odd
    blocks = grad.reshape(4, 2, grad.shape[0] // 8, grad.shape[1])
    sent = lax.dynamic_index_in_dim(blocks, 1 - odd, 1, keepdims=False)
    kept = lax.dynamic_index_in_dim(blocks, odd, 1, keepdims=False)
    pair = kept.astype(F32) + flip(sent, "fsdp", 1).astype(F32)
    pair = pair.astype(BF)
    near_chip = jnp.bitwise_xor(chip, near)
    far_chip = jnp.bitwise_xor(chip, 3 - near)
    to_far = two_way(pick(pair, jnp.bitwise_xor(chip, 3)), False)
    to_near = two_way(pick(pair, near_chip), False)
    far_sum = (pick(pair, far_chip).astype(F32) + to_far.astype(F32)).astype(BF)
    far_sum = two_way(far_sum, True)
    return pick(pair, chip).astype(F32) + to_near.astype(F32) + far_sum.astype(F32)


def scatter_tensor(blocks):
    total = blocks[0]
    for s in range(1, len(blocks)):
        total = total + shift(blocks[s].astype(BF), "tensor", -s).astype(F32)
    return total


def column_blocks(x, count):
    width = x.shape[1] // count
    return [x[:, s * width : (s + 1) * width] for s in range(count)]


def to_heads(blocks):
    return jnp.concatenate([shift(b, "tensor", -s) for s, b in enumerate(blocks)], axis=0)


def from_heads(rows):
    ranks = lax.axis_size("tensor")
    count = rows.shape[0] // ranks
    return jnp.concatenate(
        [shift(rows[s * count : (s + 1) * count], "tensor", s) for s in range(ranks)], axis=1
    )


def bias_kernel(heads, table_ref, bucket_ref, out_ref):
    group = pl.program_id(0)
    count = out_ref.shape[0]
    buckets = table_ref.shape[0]

    def some_rows(i, carry):
        rows = pl.ds(i * 32, 32)
        bucket = bucket_ref[rows, :]
        found = [jnp.zeros(bucket.shape, F32) for _ in range(count)]
        for b in range(buckets):
            here = bucket == b
            for h in range(count):
                found[h] = jnp.where(here, table_ref[b, group * count + h], found[h])
        for h in range(count):
            out_ref[h, rows, :] = found[h]
        return carry

    lax.fori_loop(0, bucket_ref.shape[0] // 32, some_rows, 0)


def window_bias(table, buckets):
    heads = table.shape[1]
    count = 4
    return pl.pallas_call(
        functools.partial(bias_kernel, heads),
        grid=(heads // count,),
        in_specs=[
            pl.BlockSpec(memory_space=pltpu.SMEM),
            pl.BlockSpec((WIN, WIN), lambda g: (0, 0)),
        ],
        out_specs=pl.BlockSpec((count, WIN, WIN), lambda g: (g, 0, 0)),
        out_shape=jax.ShapeDtypeStruct((heads, WIN, WIN), F32),
        cost_estimate=pl.CostEstimate(
            flops=40 * heads * WIN * WIN, bytes_accessed=4 * heads * WIN * WIN, transcendentals=0
        ),
    )(table, buckets)


def allowed_pairs(col_ref, row_ref):
    rows = lax.broadcasted_iota(jnp.int32, (WIN, WIN), 0)
    cols = lax.broadcasted_iota(jnp.int32, (WIN, WIN), 1)
    return (col_ref[0] == row_ref[0]) & (cols <= rows)


def self_softmax(q, k, bias, allowed):
    scores = jnp.where(allowed, nt(q, k) + bias, MASKED)
    raised = jnp.exp(scores - jnp.max(scores, axis=1, keepdims=True))
    return raised / jnp.sum(raised, axis=1, keepdims=True)


def self_forward_kernel(q_ref, k_ref, v_ref, col_ref, row_ref, bias_ref, out_ref):
    allowed = allowed_pairs(col_ref, row_ref)
    for h in range(2):
        lanes = slice(h * DH, (h + 1) * DH)
        prob = self_softmax(q_ref[:, lanes], k_ref[:, lanes], bias_ref[h], allowed)
        out_ref[:, lanes] = nn(prob.astype(BF), v_ref[:, lanes]).astype(BF)


def self_forward(qkv, ids, bias):
    rows, width = qkv.shape[0], qkv.shape[1] // 3
    pairs, windows = width // 128, rows // WIN

    def part(k):
        return pl.BlockSpec((WIN, 128), lambda g, w, k=k: (w, k * pairs + g))

    return pl.pallas_call(
        self_forward_kernel,
        grid=(pairs, windows),
        in_specs=[
            part(0),
            part(1),
            part(2),
            pl.BlockSpec((1, WIN, 1), lambda g, w: (w, 0, 0)),
            pl.BlockSpec((1, 1, WIN), lambda g, w: (w, 0, 0)),
            pl.BlockSpec((2, WIN, WIN), lambda g, w: (g, 0, 0)),
        ],
        out_specs=pl.BlockSpec((WIN, 128), lambda g, w: (w, g)),
        out_shape=jax.ShapeDtypeStruct((rows, width), BF),
        cost_estimate=pl.CostEstimate(
            flops=16 * rows * WIN * width, bytes_accessed=16 * rows * width, transcendentals=0
        ),
    )(qkv, qkv, qkv, ids.reshape(windows, WIN, 1), ids.reshape(windows, 1, WIN), bias)


def self_backward_kernel(
    q_ref, k_ref, v_ref, g_ref, col_ref, row_ref, bias_ref, bucket_ref,
    gq_ref, gk_ref, gv_ref, gb_ref, sum_ref,
):
    window, windows = pl.program_id(1), pl.num_programs(1)
    allowed = allowed_pairs(col_ref, row_ref)

    @pl.when(window == 0)
    def _():
        sum_ref[...] = jnp.zeros_like(sum_ref)

    for h in range(2):
        lanes = slice(h * DH, (h + 1) * DH)
        q, k, v, g = q_ref[:, lanes], k_ref[:, lanes], v_ref[:, lanes], g_ref[:, lanes]
        prob = self_softmax(q, k, bias_ref[h], allowed)
        prob_grad = nt(g, v)
        inner = jnp.sum(prob_grad * prob, axis=1, keepdims=True)
        score_grad = (prob * (prob_grad - inner)).astype(BF)
        gq_ref[:, lanes] = nn(score_grad, k).astype(BF)
        gk_ref[:, lanes] = tn(score_grad, q).astype(BF)
        gv_ref[:, lanes] = tn(prob.astype(BF), g).astype(BF)
        sum_ref[h] += score_grad.astype(F32)

    @pl.when(window == windows - 1)
    def _():
        def one_bucket(b, carry):
            here = bucket_ref[...] == b
            for h in range(2):
                gb_ref[h, pl.ds(b, 1), :] = jnp.sum(
                    jnp.where(here, sum_ref[h], 0.0), axis=0, keepdims=True
                )
            return carry

        lax.fori_loop(0, gb_ref.shape[1], one_bucket, 0)


def self_backward(qkv, grad, ids, bias, buckets, bucket_count):
    rows, width = qkv.shape[0], qkv.shape[1] // 3
    pairs, windows = width // 128, rows // WIN

    def part(k):
        return pl.BlockSpec((WIN, 128), lambda g, w, k=k: (w, k * pairs + g))

    return pl.pallas_call(
        self_backward_kernel,
        grid=(pairs, windows),
        in_specs=[
            part(0),
            part(1),
            part(2),
            part(0),
            pl.BlockSpec((1, WIN, 1), lambda g, w: (w, 0, 0)),
            pl.BlockSpec((1, 1, WIN), lambda g, w: (w, 0, 0)),
            pl.BlockSpec((2, WIN, WIN), lambda g, w: (g, 0, 0)),
            pl.BlockSpec((WIN, WIN), lambda g, w: (0, 0)),
        ],
        out_specs=[part(0)] * 3 + [pl.BlockSpec((2, bucket_count, WIN), lambda g, w: (g, 0, 0))],
        out_shape=[jax.ShapeDtypeStruct((rows, width), BF)] * 3
        + [jax.ShapeDtypeStruct((2 * pairs, bucket_count, WIN), F32)],
        scratch_shapes=[pltpu.VMEM((2, WIN, WIN), F32)],
        cost_estimate=pl.CostEstimate(
            flops=60 * rows * WIN * width, bytes_accessed=24 * rows * width, transcendentals=0
        ),
    )(qkv, qkv, qkv, grad, ids.reshape(windows, WIN, 1), ids.reshape(windows, 1, WIN), bias, buckets)


def cross_forward_kernel(q_ref, kv_ref, out_ref, exact_ref, total_ref, ones_ref):
    heads = q_ref.shape[1] // DH
    width = heads * DH

    @pl.when(pl.program_id(0) == 0)
    def _():
        for h in range(heads):
            values = kv_ref[:, width + h * DH : width + (h + 1) * DH]
            ones_ref[h] = jnp.concatenate([values, jnp.ones_like(values)], axis=1)

    for h in range(heads):
        lanes = slice(h * DH, (h + 1) * DH)
        scores = nt(q_ref[:, lanes], kv_ref[:, lanes])
        top = jnp.max(scores, axis=1, keepdims=True)
        raised = jnp.exp(scores - top).astype(BF)
        both = nn(raised, ones_ref[h])
        row_sum = both[:, DH:]
        context = both[:, :DH] / row_sum
        out_ref[:, lanes] = context.astype(BF)
        exact_ref[:, lanes] = context
        log_total = top + jnp.log(jnp.concatenate([row_sum, row_sum], axis=1))
        total_ref[h : h + 1, :] = jnp.transpose(log_total)[:1]


def cross_forward(queries, keys_values):
    rows, width = queries.shape
    keys = keys_values.shape[0]
    tile = WIN
    return pl.pallas_call(
        cross_forward_kernel,
        grid=(rows // tile,),
        in_specs=[
            pl.BlockSpec((tile, width), lambda i: (i, 0)),
            pl.BlockSpec((keys, 2 * width), lambda i: (0, 0)),
        ],
        out_specs=[
            pl.BlockSpec((tile, width), lambda i: (i, 0)),
            pl.BlockSpec((tile, width), lambda i: (i, 0)),
            pl.BlockSpec((8, tile), lambda i: (0, i)),
        ],
        out_shape=[
            jax.ShapeDtypeStruct((rows, width), BF),
            jax.ShapeDtypeStruct((rows, width), F32),
            jax.ShapeDtypeStruct((8, rows), F32),
        ],
        scratch_shapes=[pltpu.VMEM((width // DH, keys, 2 * DH), BF)],
        compiler_params=pltpu.CompilerParams(vmem_limit_bytes=48 * MIB),
        cost_estimate=pl.CostEstimate(
            flops=16 * rows * keys * width, bytes_accessed=4 * keys * width, transcendentals=0
        ),
    )(queries, keys_values)


def cross_backward_kernel(
    q_ref, g_ref, exact_ref, total_ref, kv_ref, gq_ref, gkv_ref, inner_ref, sum_ref
):
    step, steps = pl.program_id(0), pl.num_programs(0)
    heads = q_ref.shape[1] // DH
    width = heads * DH
    rows = q_ref.shape[0]

    @pl.when(step == 0)
    def _():
        sum_ref[...] = jnp.zeros_like(sum_ref)
        for h in range(heads):
            lanes = slice(h * DH, (h + 1) * DH)
            for first in range(0, rows, WIN):
                tile = slice(first, first + WIN)
                product = g_ref[tile, lanes].astype(F32) * exact_ref[tile, lanes]
                inner_ref[h : h + 1, tile] = jnp.sum(jnp.transpose(product), axis=0, keepdims=True)

    for h in range(heads):
        lanes = slice(h * DH, (h + 1) * DH)
        value_lanes = slice(width + h * DH, width + (h + 1) * DH)
        k, v = kv_ref[:, lanes], kv_ref[:, value_lanes]
        k_across = jnp.transpose(k)
        key_grad = jnp.zeros(k.shape, F32)
        value_grad = jnp.zeros(k.shape, F32)
        for first in range(0, rows, WIN):
            tile = slice(first, first + WIN)
            q, g = q_ref[tile, lanes], g_ref[tile, lanes]
            prob = jnp.exp(nt(k, q) - total_ref[h : h + 1, tile])
            prob_grad = nt(v, g)
            score_grad = (prob * (prob_grad - inner_ref[h : h + 1, tile])).astype(BF)
            value_grad += nn(prob.astype(BF), g)
            key_grad += nn(score_grad, q)
            sum_ref[lanes, tile] += nn(k_across, score_grad)
        gkv_ref[:, lanes] = key_grad.astype(BF)
        gkv_ref[:, value_lanes] = value_grad.astype(BF)

    @pl.when(step == steps - 1)
    def _():
        for first in range(0, rows, WIN):
            tile = slice(first, first + WIN)
            gq_ref[tile, :] = jnp.transpose(sum_ref[:, tile]).astype(BF)


def cross_backward(queries, grad, exact, total, keys_values):
    rows, width = queries.shape
    keys = keys_values.shape[0]
    tile = WIN
    whole = pl.BlockSpec((rows, width), lambda i: (0, 0))
    block = pl.BlockSpec((tile, 2 * width), lambda i: (i, 0))
    return pl.pallas_call(
        cross_backward_kernel,
        grid=(keys // tile,),
        in_specs=[whole, whole, whole, pl.BlockSpec((8, rows), lambda i: (0, 0)), block],
        out_specs=[whole, block],
        out_shape=[
            jax.ShapeDtypeStruct((rows, width), BF),
            jax.ShapeDtypeStruct((keys, 2 * width), BF),
        ],
        scratch_shapes=[pltpu.VMEM((8, rows), F32), pltpu.VMEM((width, rows), F32)],
        compiler_params=pltpu.CompilerParams(vmem_limit_bytes=48 * MIB),
        cost_estimate=pl.CostEstimate(
            flops=40 * rows * keys * width, bytes_accessed=8 * keys * width, transcendentals=0
        ),
    )(queries, grad, exact, total, keys_values)


def norm_scale(stream):
    return lax.rsqrt(jnp.mean(stream * stream, axis=-1, keepdims=True) + EPSILON)


def norm_back(stream, scale, gain, incoming):
    scaled = incoming * gain
    along = jnp.mean(scaled * stream, axis=-1, keepdims=True)
    return (
        scale * scaled - stream * (scale * scale * scale) * along,
        jnp.sum(incoming * stream * scale, axis=0, keepdims=True),
    )


def gate_and_slope(u):
    inner = 0.7978845608028654 * (u + 0.044715 * u * u * u)
    bent = jnp.tanh(inner)
    half = 0.5 * (1.0 + bent)
    slope = half + 0.5 * u * (1.0 - bent * bent) * 0.7978845608028654 * (1.0 + 0.134145 * u * u)
    return u * half, slope


def local(
    hidden, passages, block_ids, buckets, norm_gains, self_query, self_key, self_value, self_out,
    cross_query, cross_key, cross_value, cross_out, ffn_in, ffn_out, rel_bias, out_grad,
):
    ranks = lax.axis_size("tensor")
    rank = lax.axis_index("tensor")
    batches, rows, model = hidden.shape
    enc_rows = passages.shape[1]
    head_width = self_query.shape[1]
    head_count = head_width // DH
    width = head_width * ranks

    (kv_weight,) = gather_weights([cross_key, cross_value], [2 * width], True)
    qkv_weight, so_weight = gather_weights(
        [self_query, self_key, self_value, self_out], [3 * width, width], False
    )
    gains = gather_small(jnp.transpose(norm_gains))
    gains = jnp.transpose(gains, (1, 0, 2)).reshape(3, model).astype(F32)
    cq_weight, co_weight = gather_weights([cross_query, cross_out], [width, width], False)
    hidden_width = ffn_in.shape[1] * ranks
    in_weight, out_weight = gather_weights([ffn_in, ffn_out], [hidden_width, hidden_width], False)

    owners = [lax.rem(rank - s + ranks, ranks) for s in range(ranks)]
    table = jnp.concatenate(
        [lax.dynamic_slice_in_dim(rel_bias, o * head_count, head_count, 1) for o in owners], axis=1
    )
    bias = window_bias(table, buckets)
    ids = lax.dynamic_slice_in_dim(block_ids, rank * rows, rows, 1).reshape(-1, WIN)

    encoded = passages.reshape(batches * enc_rows, model)
    own_kv = nn(encoded, kv_weight).astype(BF)
    enc_kv = [
        to_heads(column_blocks(own_kv[b * enc_rows : (b + 1) * enc_rows], ranks))
        for b in range(batches)
    ]

    stream = hidden.reshape(batches * rows, model).astype(F32)
    scale_one = norm_scale(stream)
    normed_one = (stream * scale_one * gains[0]).astype(BF)
    qkv = nn(normed_one, qkv_weight).astype(BF)
    context = self_forward(qkv, ids, bias)
    after_self = stream + nt(context, so_weight)
    scale_two = norm_scale(after_self)
    normed_two = (after_self * scale_two * gains[1]).astype(BF)
    cross_rows = nn(normed_two, cq_weight).astype(BF)

    def part(x, b):
        count = x.shape[0] // batches
        return x[b * count : (b + 1) * count]

    queries = [to_heads(column_blocks(part(cross_rows, b), ranks)) for b in range(batches)]
    attended = [cross_forward(queries[b], enc_kv[b]) for b in range(batches)]
    outputs, grads_two, kept = [], [], []
    gain_three = 0.0
    for b in range(batches):
        cross_context = from_heads(attended[b][0])
        after_cross = part(after_self, b) + nt(cross_context, co_weight)
        scale_three = norm_scale(after_cross)
        normed_three = (after_cross * scale_three * gains[2]).astype(BF)
        gate, slope = gate_and_slope(nn(normed_three, in_weight))
        activated = gate.astype(BF)
        outputs.append((after_cross + nt(activated, out_weight)).astype(BF))
        incoming = out_grad[b]
        pre_grad = (nn(incoming, out_weight) * slope).astype(BF)
        normed_grad = nt(pre_grad, in_weight)
        stream_part, gain_part = norm_back(after_cross, scale_three, gains[2], normed_grad)
        gain_three = gain_three + gain_part
        grad_two = incoming.astype(F32) + stream_part
        grads_two.append(grad_two)
        kept.append((cross_context, normed_three, activated, pre_grad, grad_two.astype(BF)))
    cross_context, normed_three, activated, pre_grad, branch_two = (
        jnp.concatenate(parts, axis=0) for parts in zip(*kept)
    )
    incoming = out_grad.reshape(batches * rows, model)

    context_grads = nn(branch_two, co_weight).astype(BF)
    backs = []
    for b in range(batches):
        grad_rows = to_heads(column_blocks(part(context_grads, b), ranks))
        backs.append(cross_backward(queries[b], grad_rows, *attended[b][1:], enc_kv[b]))

    in_grad = tn(normed_three, pre_grad).astype(BF)
    out_weight_grad = tn(incoming, activated).astype(BF)
    in_sum, out_sum = scatter_fsdp(in_grad), scatter_fsdp(out_weight_grad)
    in_total = scatter_tensor(column_blocks(in_sum, ranks))
    out_total = scatter_tensor(column_blocks(out_sum, ranks))

    query_grads = jnp.concatenate([from_heads(back[0]) for back in backs], axis=0)
    normed_grad = nt(query_grads, cq_weight)
    stream_part, gain_two = norm_back(after_self, scale_two, gains[1], normed_grad)
    grad_one = jnp.concatenate(grads_two, axis=0) + stream_part
    branch_one = grad_one.astype(BF)
    context_grad = nn(branch_one, so_weight).astype(BF)
    gq, gk, gv, bias_lanes = self_backward(qkv, context_grad, ids, bias, buckets, rel_bias.shape[0])
    qkv_grad = jnp.concatenate([gq, gk, gv], axis=1)
    normed_grad = nt(qkv_grad, qkv_weight)
    stream_part, gain_one = norm_back(stream, scale_one, gains[0], normed_grad)
    input_grad = grad_one + stream_part

    kv_grad = jnp.concatenate([from_heads(back[1]) for back in backs], axis=0)
    encoded_grad = nt(kv_grad, kv_weight)
    kv_sum = scatter_fsdp(tn(encoded, kv_grad).astype(BF))
    kv_total = scatter_tensor(column_blocks(kv_sum, ranks))

    cross_grads = jnp.concatenate(
        [tn(normed_two, query_grads).astype(BF), tn(branch_two, cross_context).astype(BF)], axis=1
    )
    self_grads = jnp.concatenate(
        [tn(normed_one, qkv_grad).astype(BF), tn(branch_one, context).astype(BF)], axis=1
    )

    def split_total(summed, count):
        per_weight = [column_blocks(w, ranks) for w in column_blocks(summed, count)]
        total = scatter_tensor([jnp.concatenate(list(b), axis=1) for b in zip(*per_weight)])
        return column_blocks(total, count)

    cq_total, co_total = split_total(scatter_fsdp(cross_grads), 2)
    q_total, k_total, v_total, so_total = split_total(scatter_fsdp(self_grads), 4)

    bias_own = jnp.transpose(jnp.sum(bias_lanes, axis=2))
    bias_full = jnp.zeros(rel_bias.shape, F32)
    for s, o in enumerate(owners):
        bias_full = lax.dynamic_update_slice_in_dim(
            bias_full, bias_own[:, s * head_count : (s + 1) * head_count], o * head_count, 1
        )
    small = jnp.concatenate(
        [gain_one.reshape(-1), gain_two.reshape(-1), gain_three.reshape(-1), bias_full.reshape(-1)]
    )
    pad = -small.shape[0] % 1024
    small = jnp.pad(small, (0, pad)).reshape(8, -1)
    small = sum_everywhere(small).reshape(-1)
    gains_sum = jnp.transpose(small[: 3 * model].reshape(3, model))
    bias_total = small[3 * model : 3 * model + rel_bias.size].reshape(rel_bias.shape)

    return (
        jnp.stack(outputs),
        input_grad.reshape(batches, rows, model),
        encoded_grad.reshape(batches, enc_rows, model),
        gains_sum,
        q_total,
        k_total,
        v_total,
        so_total,
        cq_total,
        kv_total[:, :head_width],
        kv_total[:, head_width:],
        co_total,
        in_total,
        out_total,
        bias_total,
    )


def solution(mesh):
    rows = P(None, ("fsdp", "tensor"), None)
    weight = P("fsdp", "tensor")
    in_specs = (rows, rows, P(None, "fsdp"), P(), P("fsdp", None)) + (weight,) * 10 + (P(), rows)
    out_specs = (rows, rows, rows, P()) + (weight,) * 10 + (P(),)
    return jax.shard_map(local, mesh=mesh, in_specs=in_specs, out_specs=out_specs, check_vma=False)
```

```python
import functools

import jax
import jax.numpy as jnp
from jax import lax
from jax.experimental import pallas as pl
from jax.experimental.pallas import tpu as pltpu
from jax.sharding import PartitionSpec as P

DH = 64
WIN = 256
EPSILON = 1e-06
MASKED = -1000000000.0
BF = jnp.bfloat16
F32 = jnp.float32
MIB = 1024 * 1024


def nn(left, right):
    return jnp.dot(left, right, preferred_element_type=F32)


def nt(left, right):
    return lax.dot_general(left, right, (((1,), (1,)), ((), ())), preferred_element_type=F32)


def tn(left, right):
    return lax.dot_general(left, right, (((0,), (0,)), ((), ())), preferred_element_type=F32)


def shift(x, axis, by):
    size = lax.axis_size(axis)
    if by % size == 0:
        return x
    return lax.ppermute(x, axis, [(i, (i + by) % size) for i in range(size)])


def flip(x, axis, bits):
    size = lax.axis_size(axis)
    return lax.ppermute(x, axis, [(i, i ^ bits) for i in range(size)])


def two_way(x, swapped):
    first, second = (4, 2) if swapped else (2, 4)
    return lax.ppermute(x, "fsdp", [(i, i ^ (second if i & 1 else first)) for i in range(8)])


def assemble_kernel(starts, *refs):
    pieces, outs = refs[:8], refs[8:]
    me = lax.axis_index("fsdp")
    odd = lax.rem(me, 2)
    x_bit, y_bit = lax.rem(me // 2, 2), me // 4

    def flipped(dx, dy, dc):
        new_x = x_bit + dx - 2 * x_bit * dx
        new_y = y_bit + dy - 2 * y_bit * dy
        new_c = odd + dc - 2 * odd * dc
        return new_y * 4 + new_x * 2 + new_c

    even = 1 - odd
    places = [
        flipped(0, 0, 0),
        flipped(even, odd, 0),
        flipped(odd, even, 0),
        flipped(1, 1, 0),
        flipped(0, 0, 1),
        flipped(odd, even, 1),
        flipped(even, odd, 1),
        flipped(1, 1, 1),
    ]
    ranks, rows = pieces[0].shape[0], pieces[0].shape[1]
    rank = lax.axis_index("tensor")
    for place, piece in zip(places, pieces):
        here = pl.ds(pl.multiple_of(place * rows, rows), rows)
        for s in range(ranks):
            block = piece[lax.rem(rank - s + ranks, ranks)]
            for out_ref, parts in zip(outs, starts):
                for first, width, base, stride in parts:
                    out_ref[here, base + s * stride : base + s * stride + width] = block[
                        :, first : first + width
                    ]


def gather_paths(piece):
    if lax.axis_size("fsdp") != 8 or piece.shape[1] % 16:
        return [piece]
    return [piece, two_way(piece, False), two_way(piece, True)]


def gather_far(pieces):
    if len(pieces) == 1:
        return pieces
    return pieces + [two_way(pieces[1], True)]


def gather_cores(pieces):
    if len(pieces) == 1:
        return [lax.all_gather(pieces[0], "fsdp", axis=1, tiled=True)]
    return pieces + [flip(p, "fsdp", 1) for p in pieces]


def gather_end(pieces, layout, earlier=()):
    ranks, rows = pieces[0].shape[:2]
    widths = [sum(part[1] for part in parts) * ranks for parts in layout]
    if len(pieces) == 1:
        outs = []
        rank = lax.axis_index("tensor")
        order = lax.rem(rank + ranks - jnp.arange(ranks, dtype=jnp.int32), ranks)
        blocks = jnp.take(pieces[0], order, axis=0)
        for parts in layout:
            columns = {}
            for first, width, base, stride in parts:
                for s in range(ranks):
                    columns[base + s * stride] = blocks[s, :, first : first + width]
            outs.append(jnp.concatenate([columns[k] for k in sorted(columns)], axis=1))
        return outs
    return run(
        "assemble",
        functools.partial(assemble_kernel, layout),
        pieces,
        [pl.BlockSpec(memory_space=pltpu.VMEM)] * 8,
        earlier,
        sum(widths) * rows / 96000 + 1,
        out_shape=[jax.ShapeDtypeStruct((8 * rows, w), pieces[0].dtype) for w in widths],
        compiler_params=pltpu.CompilerParams(vmem_limit_bytes=48 * MIB),
    )


def run(name, kernel, operands, in_specs, earlier=(), took=1, **how):
    count = len(earlier)

    def body(*refs):
        kernel(*refs[count:])

    return pl.pallas_call(
        body,
        in_specs=[pl.BlockSpec(memory_space=pl.ANY)] * count + in_specs,
        cost_estimate=pl.CostEstimate(
            flops=int(took * 1.1e9), bytes_accessed=int(took * 3.5e6), transcendentals=0
        ),
        name=name,
        **how,
    )(*earlier, *operands)


def join_kernel(*refs):
    first = 0
    for ref in refs[:-1]:
        refs[-1][:, first : first + ref.shape[1]] = ref[...]
        first += ref.shape[1]


def joined(parts, earlier=()):
    if parts[0].shape[0] % 16:
        return beside(parts)
    return run(
        "join",
        join_kernel,
        parts,
        [pl.BlockSpec(memory_space=pltpu.VMEM)] * len(parts),
        earlier,
        1.5,
        out_shape=jax.ShapeDtypeStruct(
            (parts[0].shape[0], sum(x.shape[1] for x in parts)), parts[0].dtype
        ),
    )


def gather_ranks(shards, earlier=()):
    own = joined(shards, earlier)
    return [shift(own, "tensor", s) for s in range(lax.axis_size("tensor"))]


def gather_small(shard):
    size = lax.axis_size("fsdp")
    held = shard[None]
    bit = 1
    while bit < size:
        held = jnp.concatenate([held, flip(held, "fsdp", bit)], axis=0)
        bit *= 2
    order = jnp.bitwise_xor(jnp.arange(size, dtype=jnp.int32), lax.axis_index("fsdp"))
    return jnp.take(held, order, axis=0)


def sum_everywhere(x):
    for axis in ("fsdp", "tensor"):
        bits = []
        while 1 << len(bits) < lax.axis_size(axis):
            bits.append(1 << len(bits))
        if len(bits) % 2:
            x = x + flip(x, axis, bits.pop(0))
        for one, two in zip(bits[::2], bits[1::2]):
            x = (x + flip(x, axis, one)) + (flip(x, axis, two) + flip(x, axis, one + two))
    return x


def grad_kernel(phases, left_count, *refs):
    lefts, refs = refs[:left_count], refs[left_count:]
    outs, across_ref, rows_ref = refs[-4:-2], refs[-2], refs[-1]
    step = pl.program_id(0)
    me = lax.axis_index("fsdp")
    odd = lax.rem(me, 2)
    x_bit, y_bit = lax.rem(me // 2, 2), me // 4
    first, ref, before = 0, 0, None
    for indices, count, blocks in phases:
        rights = refs[ref : ref + count]
        ref += count

        if indices != before:

            @pl.when(step == first)
            def _(indices=indices):
                done = 0
                for i in indices:
                    across_ref[:, done : done + lefts[i].shape[0]] = jnp.transpose(lefts[i][...])
                    done += lefts[i].shape[0]

        before = indices

        @pl.when((step >= first) & (step < first + blocks))
        def _(rights=rights):
            total, done = 0.0, 0
            for right in rights:
                total = total + nn(across_ref[:, done : done + right.shape[0]], right[...])
                done += right.shape[0]
            rows_ref[...] = total.astype(BF)

        first += blocks
    size = rows_ref.shape[0] // 8
    for out_ref, core in zip(outs, (odd, 1 - odd)):
        even = 1 - core
        for place, (dx, dy) in enumerate(((0, 0), (core, even), (even, core), (1, 1))):
            block = (y_bit + dy - 2 * y_bit * dy) * 4 + (x_bit + dx - 2 * x_bit * dx) * 2 + core
            out_ref[place * size : (place + 1) * size, :] = rows_ref[
                pl.ds(pl.multiple_of(block * size, size), size), :
            ]


def weight_grads(lefts, phases, earlier=(), tile=768):
    model = lefts[0].shape[1]
    if lax.axis_size("fsdp") != 8:
        whole = []
        for indices, rights in phases:
            rights = [beside(list(y)) if y.ndim == 3 else y for y in rights]
            whole.append(tn(below([lefts[i] for i in indices]), below(rights)))
        return [beside(whole).astype(BF)]
    specs = [pl.BlockSpec(x.shape, lambda i: (0, 0)) for x in lefts]
    operands, sizes, first = list(lefts), [], 0
    for indices, rights in phases:
        deep = rights[0].ndim == 3
        count = rights[0].shape[0] if deep else rights[0].shape[1] // tile
        operands += rights
        for y in rights:
            if deep:
                shape, where = (None, y.shape[1], tile), lambda i, k: (k, 0, 0)
            else:
                shape, where = (y.shape[0], tile), lambda i, k: (0, k)
            specs.append(
                pl.BlockSpec(
                    shape,
                    lambda i, f=first, n=count, where=where: where(i, jnp.clip(i - f, 0, n - 1)),
                )
            )
        sizes.append((indices, len(rights), count))
        first += count
    deepest = max(sum(lefts[i].shape[0] for i in indices) for indices, _ in phases)
    shape = jax.ShapeDtypeStruct((model // 2, first * tile), BF)
    kept_and_sent = run(
        "weight_grads",
        functools.partial(grad_kernel, sizes, len(lefts)),
        [*operands],
        specs,
        earlier,
        first * 1.4,
        grid=(first,),
        out_specs=[pl.BlockSpec((model // 2, tile), lambda i: (0, i))] * 2,
        out_shape=[shape, shape],
        scratch_shapes=[pltpu.VMEM((model, deepest), BF), pltpu.VMEM((model, tile), BF)],
        compiler_params=pltpu.CompilerParams(vmem_limit_bytes=48 * MIB),
    )
    return list(kept_and_sent)


def rows_back_kernel(grad_ref, weight_ref, out_ref):
    out_ref[...] = nt(grad_ref[...], weight_ref[...]).astype(BF)


def rows_back(grad, weight, earlier=()):
    rows, model = grad.shape[0], weight.shape[0]
    tile = 256
    return run(
        "rows_back",
        rows_back_kernel,
        [grad, weight],
        [
            pl.BlockSpec(grad.shape, lambda i: (0, 0)),
            pl.BlockSpec((tile, weight.shape[1]), lambda i: (i, 0)),
        ],
        earlier,
        6,
        grid=(model // tile,),
        out_specs=pl.BlockSpec((rows, tile), lambda i: (0, i)),
        out_shape=jax.ShapeDtypeStruct((rows, model), BF),
        compiler_params=pltpu.CompilerParams(vmem_limit_bytes=48 * MIB),
    )


def scatter_cores(grads):
    if len(grads) == 1:
        return [lax.psum_scatter(grads[0].astype(F32), "fsdp", scatter_dimension=0, tiled=True)]
    return [grads[0], flip(grads[1], "fsdp", 1)]


def halves_kernel(kept_ref, sent_ref, low_ref, high_ref):
    half = low_ref.shape[0]
    for out_ref, rows in ((low_ref, slice(0, half)), (high_ref, slice(half, 2 * half))):
        both = kept_ref[rows, :].astype(F32) + sent_ref[rows, :].astype(F32)
        out_ref[...] = both.astype(out_ref.dtype)


def sum_halves(name, kept, received, low_type, earlier):
    rows, width = kept.shape
    tile = 768
    whole = pl.BlockSpec((rows, tile), lambda i: (0, i))
    half = pl.BlockSpec((rows // 2, tile), lambda i: (0, i))
    return run(
        name,
        halves_kernel,
        [kept, received],
        [whole, whole],
        earlier,
        rows * width / 300000,
        grid=(width // tile,),
        out_specs=[half, half],
        out_shape=[
            jax.ShapeDtypeStruct((rows // 2, width), low_type),
            jax.ShapeDtypeStruct((rows // 2, width), BF),
        ],
        compiler_params=pltpu.CompilerParams(vmem_limit_bytes=48 * MIB),
    )


def scatter_paths(stage, earlier=()):
    if len(stage) == 1:
        return stage
    low, high = sum_halves("sum_cores", *stage, BF, earlier)
    return [low, two_way(high, False)]


def scatter_far(stage, earlier=()):
    if len(stage) == 1:
        return stage
    low, high = sum_halves("sum_paths", *stage, F32, earlier)
    return [low, two_way(high, True)]


def blocks_kernel(layout, kept_ref, received_ref, out_ref):
    total = (kept_ref[...] + received_ref[...].astype(F32)).astype(BF)
    for s in range(out_ref.shape[0]):
        for first, width, base, stride in layout:
            out_ref[s, :, first : first + width] = total[
                :, base + s * stride : base + s * stride + width
            ]


def scatter_end(stage, layout, earlier=()):
    ranks = lax.axis_size("tensor")
    if len(stage) == 1:
        parts = [
            jnp.concatenate(
                [stage[0][:, b + s * d : b + s * d + w] for _, w, b, d in layout], axis=1
            )
            for s in range(ranks)
        ]
        return jnp.stack(parts).astype(BF)
    rows, width = stage[0].shape
    return run(
        "sum_far",
        functools.partial(blocks_kernel, layout),
        stage,
        [pl.BlockSpec(memory_space=pltpu.VMEM)] * 2,
        earlier,
        2,
        out_shape=jax.ShapeDtypeStruct((ranks, rows, width // ranks), BF),
        compiler_params=pltpu.CompilerParams(vmem_limit_bytes=48 * MIB),
    )


def scatter_tensor(blocks):
    parts = lax.all_to_all(blocks, "tensor", split_axis=0, concat_axis=0, tiled=True)
    return jnp.sum(parts.astype(F32), axis=0)


def column_blocks(x, count):
    width = x.shape[1] // count
    return [x[:, s * width : (s + 1) * width] for s in range(count)]


def round_moves(r, back):
    size, ranks = lax.axis_size("fsdp"), lax.axis_size("tensor")
    pairs = []
    for f in range(size):
        for t in range(ranks):
            c, t1, t0 = f & 1, t >> 1, t & 1
            pair = (f * ranks + t, ((f ^ c) | t0) * ranks + 2 * (r ^ t1) + c)
            pairs.append(pair[::-1] if back else pair)
    return pairs


def gathered(x):
    high = lax.axis_index("tensor") // 2
    parts = [
        lax.ppermute(
            lax.dynamic_index_in_dim(x, r ^ high, 0, keepdims=False),
            ("fsdp", "tensor"),
            round_moves(r, False),
        )
        for r in range(2)
    ]
    return below(parts)


def returned(x):
    half = x.shape[0] // 2
    return [
        lax.ppermute(x[r * half : (r + 1) * half], ("fsdp", "tensor"), round_moves(r, True))
        for r in range(2)
    ]


def by_batch(parts, dtype):
    high = lax.axis_index("tensor") // 2
    return jnp.stack([jnp.where(high == r, parts[0], parts[1]) for r in range(2)]).astype(dtype)


def beside(blocks):
    return jnp.concatenate(list(blocks), axis=1)


def below(blocks):
    return jnp.concatenate(list(blocks), axis=0)


def bias_kernel(heads, table_ref, bucket_ref, out_ref):
    group = pl.program_id(0)
    count = out_ref.shape[0]
    buckets = table_ref.shape[0]

    def some_rows(i, carry):
        rows = pl.ds(i * 32, 32)
        bucket = bucket_ref[rows, :]
        found = [jnp.zeros(bucket.shape, F32) for _ in range(count)]
        for b in range(buckets):
            here = bucket == b
            for h in range(count):
                found[h] = jnp.where(here, table_ref[b, group * count + h], found[h])
        for h in range(count):
            out_ref[h, rows, :] = found[h]
        return carry

    lax.fori_loop(0, bucket_ref.shape[0] // 32, some_rows, 0)


def window_bias(table, buckets, earlier=()):
    heads = table.shape[1]
    count = 4
    return run(
        "window_bias",
        functools.partial(bias_kernel, heads),
        [table, buckets],
        [
            pl.BlockSpec(memory_space=pltpu.SMEM),
            pl.BlockSpec((WIN, WIN), lambda g: (0, 0)),
        ],
        earlier,
        9,
        grid=(heads // count,),
        out_specs=pl.BlockSpec((count, WIN, WIN), lambda g: (g, 0, 0)),
        out_shape=jax.ShapeDtypeStruct((heads, WIN, WIN), F32),
    )


def allowed_pairs(col_ref, row_ref, window):
    rows = lax.broadcasted_iota(jnp.int32, (WIN, WIN), 0)
    cols = lax.broadcasted_iota(jnp.int32, (WIN, WIN), 1)
    return (col_ref[window] == row_ref[window]) & (cols <= rows)


def self_softmax(q, k, bias, allowed):
    scores = jnp.where(allowed, nt(q, k) + bias, MASKED)
    raised = jnp.exp(scores - jnp.max(scores, axis=1, keepdims=True))
    return raised / jnp.sum(raised, axis=1, keepdims=True)


def self_forward_kernel(q_ref, k_ref, v_ref, col_ref, row_ref, bias_ref, out_ref):
    for w in range(q_ref.shape[0] // WIN):
        allowed = allowed_pairs(col_ref, row_ref, w)
        rows = slice(w * WIN, (w + 1) * WIN)
        for h in range(2):
            lanes = slice(h * DH, (h + 1) * DH)
            prob = self_softmax(q_ref[rows, lanes], k_ref[rows, lanes], bias_ref[h], allowed)
            out_ref[rows, lanes] = nn(prob.astype(BF), v_ref[rows, lanes]).astype(BF)


def self_forward(qkv, ids, bias, earlier=()):
    rows, width = qkv.shape[0], qkv.shape[1] // 3
    pairs, windows = width // 128, rows // WIN

    def part(k):
        return pl.BlockSpec((rows, 128), lambda g, k=k: (0, k * pairs + g))

    return run(
        "self_forward",
        self_forward_kernel,
        [qkv, qkv, qkv, ids.reshape(windows, WIN, 1), ids.reshape(windows, 1, WIN), bias],
        [
            part(0),
            part(1),
            part(2),
            pl.BlockSpec((windows, WIN, 1), lambda g: (0, 0, 0)),
            pl.BlockSpec((windows, 1, WIN), lambda g: (0, 0, 0)),
            pl.BlockSpec((2, WIN, WIN), lambda g: (g, 0, 0)),
        ],
        earlier,
        12,
        grid=(pairs,),
        out_specs=part(0),
        out_shape=jax.ShapeDtypeStruct((rows, width), BF),
    )


def self_backward_kernel(
    q_ref, k_ref, v_ref, g_ref, col_ref, row_ref, bias_ref, gq_ref, gk_ref, gv_ref, sum_ref
):
    for w in range(q_ref.shape[0] // WIN):
        allowed = allowed_pairs(col_ref, row_ref, w)
        rows = slice(w * WIN, (w + 1) * WIN)
        for h in range(2):
            lanes = slice(h * DH, (h + 1) * DH)
            q, k, v = q_ref[rows, lanes], k_ref[rows, lanes], v_ref[rows, lanes]
            g = g_ref[rows, lanes]
            prob = self_softmax(q, k, bias_ref[h], allowed)
            prob_grad = nt(g, v)
            inner = jnp.sum(prob_grad * prob, axis=1, keepdims=True)
            score_grad = (prob * (prob_grad - inner)).astype(BF)
            gq_ref[rows, lanes] = nn(score_grad, k).astype(BF)
            gk_ref[rows, lanes] = tn(score_grad, q).astype(BF)
            gv_ref[rows, lanes] = tn(prob.astype(BF), g).astype(BF)
            if w:
                sum_ref[h] += score_grad.astype(F32)
            else:
                sum_ref[h] = score_grad.astype(F32)


def self_backward(qkv, grad, ids, bias, earlier=()):
    rows, width = qkv.shape[0], qkv.shape[1] // 3
    pairs, windows = width // 128, rows // WIN

    def part(k):
        return pl.BlockSpec((rows, 128), lambda g, k=k: (0, k * pairs + g))

    tables = pl.BlockSpec((2, WIN, WIN), lambda g: (g, 0, 0))
    return run(
        "self_backward",
        self_backward_kernel,
        [qkv, qkv, qkv, grad, ids.reshape(windows, WIN, 1), ids.reshape(windows, 1, WIN), bias],
        [
            part(0),
            part(1),
            part(2),
            part(0),
            pl.BlockSpec((windows, WIN, 1), lambda g: (0, 0, 0)),
            pl.BlockSpec((windows, 1, WIN), lambda g: (0, 0, 0)),
            tables,
        ],
        earlier,
        18,
        grid=(pairs,),
        out_specs=[part(0)] * 3 + [tables],
        out_shape=[jax.ShapeDtypeStruct((rows, width), BF)] * 3
        + [jax.ShapeDtypeStruct((2 * pairs, WIN, WIN), F32)],
    )


def bucket_kernel(sum_ref, bucket_ref, out_ref):
    def one_bucket(b, carry):
        here = bucket_ref[...] == b
        for h in range(sum_ref.shape[0]):
            out_ref[h, pl.ds(b, 1), :] = jnp.sum(
                jnp.where(here, sum_ref[h], 0.0), axis=0, keepdims=True
            )
        return carry

    lax.fori_loop(0, out_ref.shape[1], one_bucket, 0)


def bucket_sums(sums, buckets, count, earlier=()):
    heads = sums.shape[0]
    return run(
        "bucket_sums",
        bucket_kernel,
        [sums, buckets],
        [
            pl.BlockSpec((4, WIN, WIN), lambda g: (g, 0, 0)),
            pl.BlockSpec((WIN, WIN), lambda g: (0, 0)),
        ],
        earlier,
        13,
        grid=(heads // 4,),
        out_specs=pl.BlockSpec((4, count, WIN), lambda g: (g, 0, 0)),
        out_shape=jax.ShapeDtypeStruct((heads, count, WIN), F32),
    )


def cross_forward_kernel(q_ref, k0_ref, v0_ref, k1_ref, v1_ref, out_ref, exact_ref, total_ref):
    rows = q_ref.shape[0]
    for h in range(2):
        lanes = slice(h * DH, (h + 1) * DH)
        keys = [k0_ref[:, lanes], k1_ref[:, lanes]]
        values = [v0_ref[:, lanes], v1_ref[:, lanes]]
        values = [jnp.concatenate([v, jnp.ones_like(v)], axis=1) for v in values]
        for first in range(0, rows, WIN):
            tile = slice(first, first + WIN)
            scores = [nt(q_ref[tile, lanes], k) for k in keys]
            top = jnp.maximum(*[jnp.max(part, axis=1, keepdims=True) for part in scores])
            both = 0.0
            for part, v in zip(scores, values):
                both = both + nn(jnp.exp(part - top).astype(BF), v)
            row_sum = both[:, DH:]
            context = both[:, :DH] / row_sum
            out_ref[tile, lanes] = context.astype(BF)
            exact_ref[tile, lanes] = context
            log_total = top + jnp.log(jnp.concatenate([row_sum, row_sum], axis=1))
            total_ref[h : h + 1, tile] = jnp.transpose(log_total)[:1]


def cross_forward(queries, own, other, earlier=()):
    rows, width = queries.shape
    keys, pairs = own.shape[0], width // 128
    tile = pl.BlockSpec((rows, 128), lambda g: (0, g))
    left = pl.BlockSpec((keys, 128), lambda g: (0, g))
    right = pl.BlockSpec((keys, 128), lambda g: (0, pairs + g))
    return run(
        "cross_forward",
        cross_forward_kernel,
        [queries, own, own, other, other],
        [tile, left, right, left, right],
        earlier,
        26,
        grid=(pairs,),
        out_specs=[tile, tile, pl.BlockSpec((None, 8, rows), lambda g: (g, 0, 0))],
        out_shape=[
            jax.ShapeDtypeStruct((rows, width), BF),
            jax.ShapeDtypeStruct((rows, width), F32),
            jax.ShapeDtypeStruct((pairs, 8, rows), F32),
        ],
        compiler_params=pltpu.CompilerParams(vmem_limit_bytes=48 * MIB),
    )


def cross_backward_kernel(
    q_ref, g_ref, exact_ref, total_ref, k0_ref, v0_ref, k1_ref, v1_ref,
    gq_ref, gk0_ref, gv0_ref, gk1_ref, gv1_ref, inner_ref, sum_ref,
):
    step, steps = pl.program_id(1), pl.num_programs(1)
    rows = q_ref.shape[0]

    @pl.when(step == 0)
    def _():
        sum_ref[...] = jnp.zeros_like(sum_ref)
        for first in range(0, rows, WIN):
            tile = slice(first, first + WIN)
            product = jnp.transpose(g_ref[tile, :].astype(F32) * exact_ref[tile, :])
            for h in range(2):
                inner_ref[h : h + 1, tile] = jnp.sum(
                    product[h * DH : (h + 1) * DH], axis=0, keepdims=True
                )

    for k_ref, v_ref, gk_ref, gv_ref in (
        (k0_ref, v0_ref, gk0_ref, gv0_ref),
        (k1_ref, v1_ref, gk1_ref, gv1_ref),
    ):
        for h in range(2):
            lanes = slice(h * DH, (h + 1) * DH)
            k, v = k_ref[:, lanes], v_ref[:, lanes]
            k_across = jnp.transpose(k)
            key_grad = jnp.zeros(k.shape, F32)
            value_grad = jnp.zeros(k.shape, F32)
            for first in range(0, rows, WIN):
                tile = slice(first, first + WIN)
                q, g = q_ref[tile, lanes], g_ref[tile, lanes]
                prob = jnp.exp(nt(k, q) - total_ref[h : h + 1, tile])
                prob_grad = nt(v, g)
                score_grad = (prob * (prob_grad - inner_ref[h : h + 1, tile])).astype(BF)
                value_grad += nn(prob.astype(BF), g)
                key_grad += nn(score_grad, q)
                sum_ref[lanes, tile] += nn(k_across, score_grad)
            gk_ref[:, lanes] = key_grad.astype(gk_ref.dtype)
            gv_ref[:, lanes] = value_grad.astype(gv_ref.dtype)

    @pl.when(step == steps - 1)
    def _():
        for first in range(0, rows, WIN):
            tile = slice(first, first + WIN)
            gq_ref[tile, :] = jnp.transpose(sum_ref[:, tile]).astype(BF)


def cross_backward(queries, grads, exact, total, own, other, earlier=()):
    rows, width = queries.shape
    keys, pairs = own.shape[0], width // 128
    parts = 4
    tile = pl.BlockSpec((rows, 128), lambda g, j: (0, g))
    left = pl.BlockSpec((keys // parts, 128), lambda g, j: (j, g))
    right = pl.BlockSpec((keys // parts, 128), lambda g, j: (j, pairs + g))
    shape = (keys, width)
    return run(
        "cross_backward",
        cross_backward_kernel,
        [queries, grads, exact, total, own, own, other, other],
        [tile, tile, tile, pl.BlockSpec((None, 8, rows), lambda g, j: (g, 0, 0))]
        + [left, right, left, right],
        earlier,
        62,
        grid=(pairs, parts),
        out_specs=[tile, left, left, left, left],
        out_shape=[
            jax.ShapeDtypeStruct(queries.shape, BF),
            jax.ShapeDtypeStruct(shape, F32),
            jax.ShapeDtypeStruct(shape, F32),
            jax.ShapeDtypeStruct(shape, BF),
            jax.ShapeDtypeStruct(shape, BF),
        ],
        scratch_shapes=[pltpu.VMEM((8, rows), F32), pltpu.VMEM((128, rows), F32)],
        compiler_params=pltpu.CompilerParams(vmem_limit_bytes=48 * MIB),
    )


def sum_keys_kernel(k0_ref, v0_ref, k1_ref, v1_ref, out_ref):
    width = k0_ref.shape[1]
    out_ref[:, :width] = (k0_ref[...] + k1_ref[...].astype(F32)).astype(BF)
    out_ref[:, width:] = (v0_ref[...] + v1_ref[...].astype(F32)).astype(BF)


def sum_keys(own, received, earlier=()):
    rows, width = own[0].shape
    tile = rows // 4
    block = pl.BlockSpec((tile, width), lambda i: (i, 0))
    return run(
        "sum_keys",
        sum_keys_kernel,
        [*own, *received],
        [block] * 4,
        earlier,
        6,
        grid=(4,),
        out_specs=pl.BlockSpec((tile, 2 * width), lambda i: (i, 0)),
        out_shape=jax.ShapeDtypeStruct((rows, 2 * width), BF),
    )


def norm_scale(stream):
    return lax.rsqrt(jnp.mean(stream * stream, axis=-1, keepdims=True) + EPSILON)


def norm_back(stream, scale, gain, incoming):
    scaled = incoming * gain
    along = jnp.mean(scaled * stream, axis=-1, keepdims=True)
    return (
        scale * scaled - stream * (scale * scale * scale) * along,
        jnp.sum(incoming * stream * scale, axis=0, keepdims=True),
    )


def gate_and_slope(u):
    inner = 0.7978845608028654 * (u + 0.044715 * u * u * u)
    bent = jnp.tanh(inner)
    half = 0.5 * (1.0 + bent)
    slope = half + 0.5 * u * (1.0 - bent * bent) * 0.7978845608028654 * (1.0 + 0.134145 * u * u)
    return u * half, slope


def local(
    hidden, passages, block_ids, buckets, norm_gains, self_query, self_key, self_value, self_out,
    cross_query, cross_key, cross_value, cross_out, ffn_in, ffn_out, rel_bias, out_grad,
):
    ranks = lax.axis_size("tensor")
    rank = lax.axis_index("tensor")
    batches, rows, model = hidden.shape
    head_width = self_query.shape[1]
    width = head_width * ranks

    hw, ffn = head_width, ffn_in.shape[1]
    self_layout = [(k * hw, hw, k * width, hw) for k in range(5)]
    kv_layout = [(0, hw, 0, hw), (hw, hw, width, hw)]
    late_layout = [(0, ffn, 0, ffn), (ffn, ffn, ranks * ffn, ffn), (2 * ffn, hw, 2 * ranks * ffn, hw)]
    gains = gather_small(jnp.transpose(norm_gains))
    gains = jnp.transpose(gains, (1, 0, 2)).reshape(3, model).astype(F32)
    self_blocks = gather_ranks([self_query, self_key, self_value, self_out, cross_query])
    kv_blocks = gather_ranks([cross_key, cross_value])
    ids = gathered(
        lax.dynamic_slice_in_dim(block_ids, rank * rows, rows, 1).reshape(batches, -1, WIN)
    )
    stream_low = gathered(hidden)
    encoded = gathered(passages)
    bias = window_bias(rel_bias, buckets, [gains, *self_blocks, *kv_blocks])
    self_pieces = gather_cores(gather_far(gather_paths(jnp.stack(self_blocks))))
    qkv_weight, so_weight, cq_weight = gather_end(
        self_pieces,
        [self_layout[:3], [(3 * hw, hw, 0, hw)], [(4 * hw, hw, 0, hw)]],
        [bias, stream_low],
    )
    late_blocks = gather_ranks([ffn_in, ffn_out, cross_out], self_blocks + kv_blocks)
    late_paths = gather_paths(jnp.stack(late_blocks))
    kv_pieces = gather_cores(gather_far(gather_paths(jnp.stack(kv_blocks))))
    (kv_weight,) = gather_end(kv_pieces, [kv_layout], [qkv_weight])

    stream = stream_low.astype(F32)
    scale_one = norm_scale(stream)
    normed_one = (stream * scale_one * gains[0]).astype(BF)
    qkv = nn(normed_one, qkv_weight).astype(BF)
    context = self_forward(qkv, ids, bias, [kv_weight])
    after_self = stream + nt(context, so_weight)
    scale_two = norm_scale(after_self)
    normed_two = (after_self * scale_two * gains[1]).astype(BF)
    queries = nn(normed_two, cq_weight).astype(BF)

    own_kv = nn(encoded, kv_weight).astype(BF)
    other_kv = flip(own_kv, "fsdp", 1)
    late_far = gather_far(late_paths)
    cross_context, exact, total = cross_forward(queries, own_kv, other_kv, late_paths[1:])
    late_pieces = gather_cores(late_far)
    in_weight, out_weight, co_weight = gather_end(
        late_pieces,
        [[(0, ffn, 0, ffn)], [(ffn, ffn, 0, ffn)], [(2 * ffn, hw, 0, hw)]],
        [cross_context],
    )

    incoming = gathered(out_grad)
    after_cross = after_self + nt(cross_context, co_weight)
    scale_three = norm_scale(after_cross)
    normed_three = (after_cross * scale_three * gains[2]).astype(BF)
    gate, slope = gate_and_slope(nn(normed_three, in_weight))
    activated = gate.astype(BF)
    output = (after_cross + nt(activated, out_weight)).astype(BF)
    pre_grad = (nn(incoming, out_weight) * slope).astype(BF)
    normed_grad = nt(pre_grad, in_weight)
    stream_part, gain_three = norm_back(after_cross, scale_three, gains[2], normed_grad)
    grad_two = incoming.astype(F32) + stream_part
    branch_two = grad_two.astype(BF)
    context_grad = nn(branch_two, co_weight).astype(BF)
    late_grads = weight_grads(
        [normed_three, incoming, branch_two],
        [((0,), [pre_grad]), ((1,), [activated]), ((2,), [cross_context])],
        [context_grad],
    )
    late_stage = scatter_cores(late_grads)

    query_grad, key_own, value_own, key_other, value_other = cross_backward(
        queries, context_grad, exact, total, own_kv, other_kv, [late_grads[0], output]
    )
    output = returned(output)
    kv_received = [flip(x, "fsdp", 1) for x in (key_other, value_other)]
    late_stage = scatter_paths(late_stage, [query_grad])
    normed_grad = nt(query_grad, cq_weight)
    stream_part, gain_two = norm_back(after_self, scale_two, gains[1], normed_grad)
    grad_one = grad_two + stream_part
    branch_one = grad_one.astype(BF)
    context_grad = nn(branch_one, so_weight).astype(BF)
    kv_grad = sum_keys([key_own, value_own], kv_received, [late_stage[0]])
    encoded_grad = rows_back(kv_grad, kv_weight)
    encoded_grads = returned(encoded_grad)

    gq, gk, gv, sums = self_backward(qkv, context_grad, ids, bias, [encoded_grad, *late_stage[1:]])
    late_stage = scatter_far(late_stage, [gq])
    self_grads = weight_grads(
        [normed_one, branch_one, normed_two],
        [((0,), [gq]), ((0,), [gk]), ((0,), [gv]), ((1,), [context]), ((2,), [query_grad])],
        late_stage[:1],
    )
    self_stage = scatter_cores(self_grads)
    kv_sums = weight_grads([encoded], [((0,), [kv_grad])], [self_grads[0]])
    kv_stage = scatter_cores(kv_sums)
    late_blocks = scatter_end(late_stage, late_layout, [kv_sums[0]])
    self_stage = scatter_paths(self_stage, [late_blocks])
    kv_stage = scatter_paths(kv_stage, [self_stage[0]])
    late_total = scatter_tensor(late_blocks)
    in_total, out_total, co_total = late_total[:, :ffn], late_total[:, ffn : 2 * ffn], late_total[:, 2 * ffn :]
    normed_grad = sum(nt(x, qkv_weight[:, k * width : (k + 1) * width]) for k, x in enumerate((gq, gk, gv)))
    stream_part, gain_one = norm_back(stream, scale_one, gains[0], normed_grad)
    input_grads = returned((grad_one + stream_part).astype(BF))
    bias_lanes = bucket_sums(sums, buckets, rel_bias.shape[0], [kv_stage[0]])
    self_stage = scatter_far(self_stage, [bias_lanes])
    kv_stage = scatter_far(kv_stage, [self_stage[0]])
    self_total = scatter_tensor(scatter_end(self_stage, self_layout, [kv_stage[0]]))
    q_total, k_total, v_total, so_total, cq_total = column_blocks(self_total, 5)
    kv_total = scatter_tensor(scatter_end(kv_stage, kv_layout, [kv_stage[0]]))

    bias_own = jnp.transpose(jnp.sum(bias_lanes, axis=2))
    small = jnp.concatenate(
        [gain_one.reshape(-1), gain_two.reshape(-1), gain_three.reshape(-1), bias_own.reshape(-1)]
    )
    pad = -small.shape[0] % 1024
    small = jnp.pad(small, (0, pad)).reshape(8, -1)
    small = sum_everywhere(small).reshape(-1)
    gains_sum = jnp.transpose(small[: 3 * model].reshape(3, model))
    bias_total = small[3 * model : 3 * model + rel_bias.size].reshape(rel_bias.shape)

    return (
        by_batch(output, BF),
        by_batch(input_grads, F32),
        by_batch(encoded_grads, F32),
        gains_sum,
        q_total,
        k_total,
        v_total,
        so_total,
        cq_total,
        kv_total[:, :head_width],
        kv_total[:, head_width:],
        co_total,
        in_total,
        out_total,
        bias_total,
    )


def solution(mesh):
    rows = P(None, ("fsdp", "tensor"), None)
    weight = P("fsdp", "tensor")
    in_specs = (rows, rows, P(None, "fsdp"), P(), P("fsdp", None)) + (weight,) * 10 + (P(), rows)
    out_specs = (rows, rows, rows, P()) + (weight,) * 10 + (P(),)
    return jax.shard_map(local, mesh=mesh, in_specs=in_specs, out_specs=out_specs, check_vma=False)
```

```python
import functools

import jax
import jax.numpy as jnp
from jax import lax
from jax.experimental import pallas as pl
from jax.experimental.pallas import tpu as pltpu
from jax.sharding import PartitionSpec as P

DH = 64
WIN = 256
EPSILON = 1e-06
MASKED = -1000000000.0
BF = jnp.bfloat16
F32 = jnp.float32
MIB = 1024 * 1024
TOOK = {'assemble': 1, 'self_forward': 1, 'self_backward': 1, 'weight_grads': 0.5, 'sum_keys': 1, 'rows_back': 1, 'sum_far': 1, 'spread': 1, 'pick_with_ids': 1, 'pick': 1, 'join': 1, 'window_bias': 1, 'cross_forward': 1, 'cross_backward': 1, 'bucket_sums': 1, 'sum_cores': 1, 'sum_paths': 2, 'feed_forward': 1, 'norm_back': 1, 'stack': 1, 'project': 1}
OPT = {'T': 0, 'Q': 1, 'R': 0, 'S': 0, 'A': 0, 'B': 1, 'C': 0, 'D': 1, 'E': 0, 'F': 1, 'G': 0, 'H': 0, 'I': 0, 'J': 0, 'K': 0, 'L': 2, 'M': 0, 'N': 0, 'P': 1}


def nn(left, right):
    return jnp.dot(left, right, preferred_element_type=F32)


def nt(left, right):
    return lax.dot_general(left, right, (((1,), (1,)), ((), ())), preferred_element_type=F32)


def tn(left, right):
    return lax.dot_general(left, right, (((0,), (0,)), ((), ())), preferred_element_type=F32)


def shift(x, axis, by):
    size = lax.axis_size(axis)
    if by % size == 0:
        return x
    return lax.ppermute(x, axis, [(i, (i + by) % size) for i in range(size)])


def flip(x, axis, bits):
    size = lax.axis_size(axis)
    return lax.ppermute(x, axis, [(i, i ^ bits) for i in range(size)])


def two_way(x, swapped):
    first, second = (4, 2) if swapped else (2, 4)
    return lax.ppermute(x, "fsdp", [(i, i ^ (second if i & 1 else first)) for i in range(8)])


def assemble_kernel(starts, by_distance, *refs):
    pieces, outs = refs[:8], refs[8:]
    me = lax.axis_index("fsdp")
    odd = lax.rem(me, 2)
    x_bit, y_bit = lax.rem(me // 2, 2), me // 4

    def flipped(dx, dy, dc):
        new_x = x_bit + dx - 2 * x_bit * dx
        new_y = y_bit + dy - 2 * y_bit * dy
        new_c = odd + dc - 2 * odd * dc
        return new_y * 4 + new_x * 2 + new_c

    even = 1 - odd
    places = [
        flipped(0, 0, 0),
        flipped(even, odd, 0),
        flipped(odd, even, 0),
        flipped(1, 1, 0),
        flipped(0, 0, 1),
        flipped(odd, even, 1),
        flipped(even, odd, 1),
        flipped(1, 1, 1),
    ]
    ranks, rows = pieces[0].shape[0], pieces[0].shape[1]
    rank = lax.axis_index("tensor")
    for place, piece in zip(places, pieces):
        here = pl.ds(pl.multiple_of(place * rows, rows), rows)
        for s in range(ranks):
            block = piece[lax.rem(rank - s + ranks, ranks) if by_distance else s]
            for out_ref, parts in zip(outs, starts):
                for first, width, base, stride in parts:
                    out_ref[here, base + s * stride : base + s * stride + width] = block[
                        :, first : first + width
                    ]


def gather_paths(piece):
    if lax.axis_size("fsdp") != 8 or piece.shape[1] % 16:
        return [piece]
    return [piece, two_way(piece, False), two_way(piece, True)]


def gather_far(pieces):
    if len(pieces) == 1:
        return pieces
    return pieces + [two_way(pieces[1], True)]


def gather_cores(pieces):
    if len(pieces) == 1:
        return [lax.all_gather(pieces[0], "fsdp", axis=1, tiled=True)]
    return pieces + [flip(p, "fsdp", 1) for p in pieces]


def gather_end(pieces, layout, earlier=(), by_distance=True):
    ranks, rows = pieces[0].shape[:2]
    widths = [sum(part[1] for part in parts) * ranks for parts in layout]
    if len(pieces) == 1:
        outs = []
        rank = lax.axis_index("tensor")
        order = lax.rem(rank + ranks - jnp.arange(ranks, dtype=jnp.int32), ranks)
        blocks = jnp.take(pieces[0], order, axis=0) if by_distance else pieces[0]
        for parts in layout:
            columns = {}
            for first, width, base, stride in parts:
                for s in range(ranks):
                    columns[base + s * stride] = blocks[s, :, first : first + width]
            outs.append(jnp.concatenate([columns[k] for k in sorted(columns)], axis=1))
        return outs
    return run(
        "assemble",
        functools.partial(assemble_kernel, layout, by_distance),
        pieces,
        [pl.BlockSpec(memory_space=pltpu.VMEM)] * 8,
        earlier,
        sum(widths) * rows / 96000 + 1,
        out_shape=[jax.ShapeDtypeStruct((8 * rows, w), pieces[0].dtype) for w in widths],
        compiler_params=pltpu.CompilerParams(vmem_limit_bytes=48 * MIB),
    )


def run(name, kernel, operands, in_specs, earlier=(), took=1, **how):
    count, took = len(earlier), took * TOOK[name]

    def body(*refs):
        kernel(*refs[count:])

    return pl.pallas_call(
        body,
        in_specs=[pl.BlockSpec(memory_space=pl.ANY)] * count + in_specs,
        cost_estimate=pl.CostEstimate(
            flops=int(took * 1.1e9), bytes_accessed=int(took * 3.5e6), transcendentals=0
        ),
        name=name,
        **how,
    )(*earlier, *operands)


def join_kernel(*refs):
    first = 0
    for ref in refs[:-1]:
        refs[-1][:, first : first + ref.shape[1]] = ref[...]
        first += ref.shape[1]


def joined(parts, earlier=()):
    if parts[0].shape[0] % 16:
        return beside(parts)
    return run(
        "join",
        join_kernel,
        parts,
        [pl.BlockSpec(memory_space=pltpu.VMEM)] * len(parts),
        earlier,
        1.5,
        out_shape=jax.ShapeDtypeStruct(
            (parts[0].shape[0], sum(x.shape[1] for x in parts)), parts[0].dtype
        ),
    )


def spread_kernel(*refs):
    out_ref, first = refs[-1], 0
    for ref in refs[:-1]:
        for s in range(out_ref.shape[0]):
            out_ref[s, :, first : first + ref.shape[1]] = ref[...]
        first += ref.shape[1]


def gather_ranks_at_once(shards, earlier=()):
    ranks, rows = lax.axis_size("tensor"), shards[0].shape[0]
    width = sum(x.shape[1] for x in shards)
    if rows % 16:
        return lax.all_gather(beside(shards), "tensor", axis=0)
    copies = run(
        "spread",
        spread_kernel,
        shards,
        [pl.BlockSpec(memory_space=pltpu.VMEM)] * len(shards),
        earlier,
        out_shape=jax.ShapeDtypeStruct((ranks, rows, width), shards[0].dtype),
    )
    return lax.all_to_all(copies, "tensor", split_axis=0, concat_axis=0, tiled=True)


def gather_ranks(shards, earlier=()):
    own = joined(shards, earlier)
    return [shift(own, "tensor", s) for s in range(lax.axis_size("tensor"))]


def gather_small(shard):
    size = lax.axis_size("fsdp")
    held = shard[None]
    bit = 1
    while bit < size:
        held = jnp.concatenate([held, flip(held, "fsdp", bit)], axis=0)
        bit *= 2
    order = jnp.bitwise_xor(jnp.arange(size, dtype=jnp.int32), lax.axis_index("fsdp"))
    return jnp.take(held, order, axis=0)


def sum_everywhere(x):
    for axis in ("fsdp", "tensor"):
        bits = []
        while 1 << len(bits) < lax.axis_size(axis):
            bits.append(1 << len(bits))
        if len(bits) % 2:
            x = x + flip(x, axis, bits.pop(0))
        for one, two in zip(bits[::2], bits[1::2]):
            x = (x + flip(x, axis, one)) + (flip(x, axis, two) + flip(x, axis, one + two))
    return x


def grad_kernel(phases, left_count, *refs):
    lefts, refs = refs[:left_count], refs[left_count:]
    outs, across_ref, rows_ref = refs[-4:-2], refs[-2], refs[-1]
    step = pl.program_id(0)
    me = lax.axis_index("fsdp")
    odd = lax.rem(me, 2)
    x_bit, y_bit = lax.rem(me // 2, 2), me // 4
    first, ref, before = 0, 0, None
    for indices, count, blocks in phases:
        rights = refs[ref : ref + count]
        ref += count

        if indices != before:

            @pl.when(step == first)
            def _(indices=indices):
                done = 0
                for i in indices:
                    across_ref[:, done : done + lefts[i].shape[0]] = jnp.transpose(lefts[i][...])
                    done += lefts[i].shape[0]

        before = indices

        @pl.when((step >= first) & (step < first + blocks))
        def _(rights=rights):
            total, done = 0.0, 0
            for right in rights:
                total = total + nn(across_ref[:, done : done + right.shape[0]], right[...])
                done += right.shape[0]
            rows_ref[...] = total.astype(BF)

        first += blocks
    size = rows_ref.shape[0] // 8
    for out_ref, core in zip(outs, (odd, 1 - odd)):
        even = 1 - core
        for place, (dx, dy) in enumerate(((0, 0), (core, even), (even, core), (1, 1))):
            block = (y_bit + dy - 2 * y_bit * dy) * 4 + (x_bit + dx - 2 * x_bit * dx) * 2 + core
            out_ref[place * size : (place + 1) * size, :] = rows_ref[
                pl.ds(pl.multiple_of(block * size, size), size), :
            ]


def weight_grads(lefts, phases, earlier=(), tile=768):
    model = lefts[0].shape[1]
    if lax.axis_size("fsdp") != 8:
        whole = []
        for indices, rights in phases:
            rights = [beside(list(y)) if y.ndim == 3 else y for y in rights]
            whole.append(tn(below([lefts[i] for i in indices]), below(rights)))
        return [beside(whole).astype(BF)]
    specs = [pl.BlockSpec(x.shape, lambda i: (0, 0)) for x in lefts]
    operands, sizes, first = list(lefts), [], 0
    for indices, rights in phases:
        deep = rights[0].ndim == 3
        count = rights[0].shape[0] if deep else rights[0].shape[1] // tile
        operands += rights
        for y in rights:
            if deep:
                shape, where = (None, y.shape[1], tile), lambda i, k: (k, 0, 0)
            else:
                shape, where = (y.shape[0], tile), lambda i, k: (0, k)
            specs.append(
                pl.BlockSpec(
                    shape,
                    lambda i, f=first, n=count, where=where: where(i, jnp.clip(i - f, 0, n - 1)),
                )
            )
        sizes.append((indices, len(rights), count))
        first += count
    deepest = max(sum(lefts[i].shape[0] for i in indices) for indices, _ in phases)
    shape = jax.ShapeDtypeStruct((model // 2, first * tile), BF)
    kept_and_sent = run(
        "weight_grads",
        functools.partial(grad_kernel, sizes, len(lefts)),
        [*operands],
        specs,
        earlier,
        first * 1.4,
        grid=(first,),
        out_specs=[pl.BlockSpec((model // 2, tile), lambda i: (0, i))] * 2,
        out_shape=[shape, shape],
        scratch_shapes=[pltpu.VMEM((model, deepest), BF), pltpu.VMEM((model, tile), BF)],
        compiler_params=pltpu.CompilerParams(vmem_limit_bytes=48 * MIB),
    )
    return list(kept_and_sent)


def rows_back_kernel(grad_ref, weight_ref, low_ref, high_ref):
    half = low_ref.shape[0]
    low_ref[...] = nt(grad_ref[:half], weight_ref[...]).astype(BF)
    high_ref[...] = nt(grad_ref[half:], weight_ref[...]).astype(BF)


def rows_back(grad, weight, earlier=()):
    rows, model = grad.shape[0], weight.shape[0]
    tile = 256
    return run(
        "rows_back",
        rows_back_kernel,
        [grad, weight],
        [
            pl.BlockSpec(grad.shape, lambda i: (0, 0)),
            pl.BlockSpec((tile, weight.shape[1]), lambda i: (i, 0)),
        ],
        earlier,
        6,
        grid=(model // tile,),
        out_specs=[pl.BlockSpec((rows // 2, tile), lambda i: (0, i))] * 2,
        out_shape=[jax.ShapeDtypeStruct((rows // 2, model), BF)] * 2,
        compiler_params=pltpu.CompilerParams(vmem_limit_bytes=48 * MIB),
    )


def scatter_cores(grads):
    if len(grads) == 1:
        return [lax.psum_scatter(grads[0].astype(F32), "fsdp", scatter_dimension=0, tiled=True)]
    return [grads[0], flip(grads[1], "fsdp", 1)]


def halves_kernel(kept_ref, sent_ref, low_ref, high_ref):
    half = low_ref.shape[0]
    for out_ref, rows in ((low_ref, slice(0, half)), (high_ref, slice(half, 2 * half))):
        both = kept_ref[rows, :].astype(F32) + sent_ref[rows, :].astype(F32)
        out_ref[...] = both.astype(out_ref.dtype)


def sum_halves(name, kept, received, low_type, earlier):
    rows, width = kept.shape
    tile = 768
    whole = pl.BlockSpec((rows, tile), lambda i: (0, i))
    half = pl.BlockSpec((rows // 2, tile), lambda i: (0, i))
    return run(
        name,
        halves_kernel,
        [kept, received],
        [whole, whole],
        earlier,
        rows * width / 300000,
        grid=(width // tile,),
        out_specs=[half, half],
        out_shape=[
            jax.ShapeDtypeStruct((rows // 2, width), low_type),
            jax.ShapeDtypeStruct((rows // 2, width), BF),
        ],
        compiler_params=pltpu.CompilerParams(vmem_limit_bytes=48 * MIB),
    )


def scatter_paths(stage, earlier=()):
    if len(stage) == 1:
        return stage
    low, high = sum_halves("sum_cores", *stage, BF, earlier)
    return [low, two_way(high, False)]


def scatter_far(stage, earlier=()):
    if len(stage) == 1:
        return stage
    low, high = sum_halves("sum_paths", *stage, F32, earlier)
    return [low, two_way(high, True)]


def blocks_kernel(layout, kept_ref, received_ref, out_ref):
    total = (kept_ref[...] + received_ref[...].astype(F32)).astype(BF)
    for s in range(out_ref.shape[0]):
        for first, width, base, stride in layout:
            out_ref[s, :, first : first + width] = total[
                :, base + s * stride : base + s * stride + width
            ]


def scatter_end(stage, layout, earlier=()):
    ranks = lax.axis_size("tensor")
    if len(stage) == 1:
        parts = [
            jnp.concatenate(
                [stage[0][:, b + s * d : b + s * d + w] for _, w, b, d in layout], axis=1
            )
            for s in range(ranks)
        ]
        return jnp.stack(parts).astype(BF)
    rows, width = stage[0].shape
    return run(
        "sum_far",
        functools.partial(blocks_kernel, layout),
        stage,
        [pl.BlockSpec(memory_space=pltpu.VMEM)] * 2,
        earlier,
        2,
        out_shape=jax.ShapeDtypeStruct((ranks, rows, width // ranks), BF),
        compiler_params=pltpu.CompilerParams(vmem_limit_bytes=48 * MIB),
    )


def scatter_tensor(blocks):
    parts = lax.all_to_all(blocks, "tensor", split_axis=0, concat_axis=0, tiled=True)
    return jnp.sum(parts.astype(F32), axis=0)


def column_blocks(x, count):
    width = x.shape[1] // count
    return [x[:, s * width : (s + 1) * width] for s in range(count)]


def round_moves(r, back):
    size, ranks = lax.axis_size("fsdp"), lax.axis_size("tensor")
    pairs = []
    for f in range(size):
        for t in range(ranks):
            c, t1, t0 = f & 1, t >> 1, t & 1
            pair = (f * ranks + t, ((f ^ c) | t0) * ranks + 2 * (r ^ t1) + c)
            pairs.append(pair[::-1] if back else pair)
    return pairs


def pick_with_ids_kernel(x_ref, ids_ref, *outs):
    high = lax.axis_index("tensor") // 2
    rows = x_ref.shape[1]
    for r, out_ref in enumerate(outs):
        b = high + r - 2 * high * r
        out_ref[:rows] = x_ref[b]
        out_ref[rows:] = jnp.zeros((out_ref.shape[0] - rows, x_ref.shape[2]), BF)
        for w in range(rows // WIN):
            place = lax.rem(ids_ref[b, w], WIN).astype(F32).astype(BF)
            out_ref[rows + 16 * w : rows + 16 * (w + 1), :WIN] = jnp.broadcast_to(place, (16, WIN))


def gathered_with_ids(x, ids, earlier=()):
    rows, width = x.shape[1:]
    windows = rows // WIN
    parts = run(
        "pick_with_ids",
        pick_with_ids_kernel,
        [x, ids.reshape(ids.shape[0], windows, 1, WIN)],
        [pl.BlockSpec(memory_space=pltpu.VMEM)] * 2,
        earlier,
        out_shape=[jax.ShapeDtypeStruct((rows + 16 * windows, width), BF)] * 2,
    )
    moved = [lax.ppermute(y, ("fsdp", "tensor"), round_moves(r, False)) for r, y in enumerate(parts)]
    places = [y[rows + 16 * w : rows + 16 * w + 1, :WIN] for y in moved for w in range(windows)]
    return below([y[:rows] for y in moved]), below(places).astype(jnp.int32), moved, parts[:1]


def gathered(x):
    high = lax.axis_index("tensor") // 2
    parts = [
        lax.ppermute(
            lax.dynamic_index_in_dim(x, r ^ high, 0, keepdims=False),
            ("fsdp", "tensor"),
            round_moves(r, False),
        )
        for r in range(2)
    ]
    return below(parts)


def pick_kernel(x_ref, *outs):
    high = lax.axis_index("tensor") // 2
    for r, out_ref in enumerate(outs):
        out_ref[...] = x_ref[high + r - 2 * high * r]


def pick_with_ids_kernel(x_ref, ids_ref, *outs):
    high = lax.axis_index("tensor") // 2
    rows = x_ref.shape[1]
    for r, out_ref in enumerate(outs):
        b = high + r - 2 * high * r
        out_ref[:rows] = x_ref[b]
        out_ref[rows:] = jnp.zeros((out_ref.shape[0] - rows, x_ref.shape[2]), BF)
        for w in range(rows // WIN):
            place = lax.rem(ids_ref[b, w], WIN).astype(F32).astype(BF)
            out_ref[rows + 16 * w : rows + 16 * (w + 1), :WIN] = jnp.broadcast_to(place, (16, WIN))


def gathered_with_ids(x, ids, earlier=()):
    rows, width = x.shape[1:]
    windows = rows // WIN
    parts = run(
        "pick_with_ids",
        pick_with_ids_kernel,
        [x, ids.reshape(ids.shape[0], windows, 1, WIN)],
        [pl.BlockSpec(memory_space=pltpu.VMEM)] * 2,
        earlier,
        out_shape=[jax.ShapeDtypeStruct((rows + 16 * windows, width), BF)] * 2,
    )
    moved = [lax.ppermute(y, ("fsdp", "tensor"), round_moves(r, False)) for r, y in enumerate(parts)]
    places = [y[rows + 16 * w : rows + 16 * w + 1, :WIN] for y in moved for w in range(windows)]
    return below([y[:rows] for y in moved]), below(places).astype(jnp.int32), moved, parts[:1]


def gathered_after(x, earlier):
    parts = run(
        "pick",
        pick_kernel,
        [x],
        [pl.BlockSpec(memory_space=pltpu.VMEM)],
        earlier,
        out_shape=[jax.ShapeDtypeStruct(x.shape[1:], x.dtype)] * 2,
        compiler_params=pltpu.CompilerParams(vmem_limit_bytes=48 * MIB),
    )
    moved = [lax.ppermute(y, ("fsdp", "tensor"), round_moves(r, False)) for r, y in enumerate(parts)]
    return below(moved)


def returned(parts):
    return [
        lax.ppermute(x, ("fsdp", "tensor"), round_moves(r, True)) for r, x in enumerate(parts)
    ]


def by_batch(parts, dtype):
    high = lax.axis_index("tensor") // 2
    return jnp.stack([jnp.where(high == r, parts[0], parts[1]) for r in range(2)]).astype(dtype)


def beside(blocks):
    return jnp.concatenate(list(blocks), axis=1)


def below(blocks):
    return jnp.concatenate(list(blocks), axis=0)


def bias_kernel(heads, table_ref, bucket_ref, out_ref):
    group = pl.program_id(0)
    count = out_ref.shape[0]
    buckets = table_ref.shape[0]

    def some_rows(i, carry):
        rows = pl.ds(i * 32, 32)
        bucket = bucket_ref[rows, :]
        found = [jnp.zeros(bucket.shape, F32) for _ in range(count)]
        for b in range(buckets):
            here = bucket == b
            for h in range(count):
                found[h] = jnp.where(here, table_ref[b, group * count + h], found[h])
        for h in range(count):
            out_ref[h, rows, :] = found[h]
        return carry

    lax.fori_loop(0, bucket_ref.shape[0] // 32, some_rows, 0)


def window_bias(table, buckets, earlier=()):
    heads = table.shape[1]
    count = 4
    return run(
        "window_bias",
        functools.partial(bias_kernel, heads),
        [table, buckets],
        [
            pl.BlockSpec(memory_space=pltpu.SMEM),
            pl.BlockSpec((WIN, WIN), lambda g: (0, 0)),
        ],
        earlier,
        9,
        grid=(heads // count,),
        out_specs=pl.BlockSpec((count, WIN, WIN), lambda g: (g, 0, 0)),
        out_shape=jax.ShapeDtypeStruct((heads, WIN, WIN), F32),
    )


def allowed_pairs(col_ref, row_ref, window):
    rows = lax.broadcasted_iota(jnp.int32, (WIN, WIN), 0)
    cols = lax.broadcasted_iota(jnp.int32, (WIN, WIN), 1)
    return (col_ref[window] == row_ref[window]) & (cols <= rows)


def self_softmax(q, k, bias, allowed):
    scores = jnp.where(allowed, nt(q, k) + bias, MASKED)
    raised = jnp.exp(scores - jnp.max(scores, axis=1, keepdims=True))
    return raised / jnp.sum(raised, axis=1, keepdims=True)


def self_forward_kernel(q_ref, k_ref, v_ref, col_ref, row_ref, bias_ref, out_ref):
    for w in range(q_ref.shape[0] // WIN):
        allowed = allowed_pairs(col_ref, row_ref, w)
        rows = slice(w * WIN, (w + 1) * WIN)
        for h in range(2):
            lanes = slice(h * DH, (h + 1) * DH)
            prob = self_softmax(q_ref[rows, lanes], k_ref[rows, lanes], bias_ref[h], allowed)
            out_ref[rows, lanes] = nn(prob.astype(BF), v_ref[rows, lanes]).astype(BF)


def self_forward(qkv, ids, bias, earlier=()):
    rows, width = qkv.shape[0], qkv.shape[1] // 3
    pairs, windows = width // 128, rows // WIN

    def part(k):
        return pl.BlockSpec((rows, 128), lambda g, k=k: (0, k * pairs + g))

    return run(
        "self_forward",
        self_forward_kernel,
        [qkv, qkv, qkv, ids.reshape(windows, WIN, 1), ids.reshape(windows, 1, WIN), bias],
        [
            part(0),
            part(1),
            part(2),
            pl.BlockSpec((windows, WIN, 1), lambda g: (0, 0, 0)),
            pl.BlockSpec((windows, 1, WIN), lambda g: (0, 0, 0)),
            pl.BlockSpec((2, WIN, WIN), lambda g: (g, 0, 0)),
        ],
        earlier,
        12,
        grid=(pairs,),
        out_specs=part(0),
        out_shape=jax.ShapeDtypeStruct((rows, width), BF),
    )


def self_backward_kernel(
    q_ref, k_ref, v_ref, g_ref, col_ref, row_ref, bias_ref, gq_ref, gk_ref, gv_ref, sum_ref
):
    for w in range(q_ref.shape[0] // WIN):
        allowed = allowed_pairs(col_ref, row_ref, w)
        rows = slice(w * WIN, (w + 1) * WIN)
        for h in range(2):
            lanes = slice(h * DH, (h + 1) * DH)
            q, k, v = q_ref[rows, lanes], k_ref[rows, lanes], v_ref[rows, lanes]
            g = g_ref[rows, lanes]
            prob = self_softmax(q, k, bias_ref[h], allowed)
            prob_grad = nt(g, v)
            inner = jnp.sum(prob_grad * prob, axis=1, keepdims=True)
            score_grad = (prob * (prob_grad - inner)).astype(BF)
            gq_ref[rows, lanes] = nn(score_grad, k).astype(BF)
            gk_ref[rows, lanes] = tn(score_grad, q).astype(BF)
            gv_ref[rows, lanes] = tn(prob.astype(BF), g).astype(BF)
            if w:
                sum_ref[h] += score_grad.astype(F32)
            else:
                sum_ref[h] = score_grad.astype(F32)


def self_backward(qkv, grad, ids, bias, earlier=()):
    rows, width = qkv.shape[0], qkv.shape[1] // 3
    pairs, windows = width // 128, rows // WIN

    def part(k):
        return pl.BlockSpec((rows, 128), lambda g, k=k: (0, k * pairs + g))

    tables = pl.BlockSpec((2, WIN, WIN), lambda g: (g, 0, 0))
    return run(
        "self_backward",
        self_backward_kernel,
        [qkv, qkv, qkv, grad, ids.reshape(windows, WIN, 1), ids.reshape(windows, 1, WIN), bias],
        [
            part(0),
            part(1),
            part(2),
            part(0),
            pl.BlockSpec((windows, WIN, 1), lambda g: (0, 0, 0)),
            pl.BlockSpec((windows, 1, WIN), lambda g: (0, 0, 0)),
            tables,
        ],
        earlier,
        18,
        grid=(pairs,),
        out_specs=[part(0)] * 3 + [tables],
        out_shape=[jax.ShapeDtypeStruct((rows, width), BF)] * 3
        + [jax.ShapeDtypeStruct((2 * pairs, WIN, WIN), F32)],
    )


def bucket_kernel(sum_ref, bucket_ref, out_ref):
    def one_bucket(b, carry):
        here = bucket_ref[...] == b
        for h in range(sum_ref.shape[0]):
            out_ref[h, pl.ds(b, 1), :] = jnp.sum(
                jnp.where(here, sum_ref[h], 0.0), axis=0, keepdims=True
            )
        return carry

    lax.fori_loop(0, out_ref.shape[1], one_bucket, 0)


def bucket_sums(sums, buckets, count, earlier=()):
    heads = sums.shape[0]
    return run(
        "bucket_sums",
        bucket_kernel,
        [sums, buckets],
        [
            pl.BlockSpec((4, WIN, WIN), lambda g: (g, 0, 0)),
            pl.BlockSpec((WIN, WIN), lambda g: (0, 0)),
        ],
        earlier,
        13,
        grid=(heads // 4,),
        out_specs=pl.BlockSpec((4, count, WIN), lambda g: (g, 0, 0)),
        out_shape=jax.ShapeDtypeStruct((heads, count, WIN), F32),
    )


def cross_forward_kernel(q_ref, k0_ref, v0_ref, k1_ref, v1_ref, out_ref, exact_ref, total_ref):
    rows = q_ref.shape[0]
    for h in range(2):
        lanes = slice(h * DH, (h + 1) * DH)
        keys = [k0_ref[:, lanes], k1_ref[:, lanes]]
        values = [v0_ref[:, lanes], v1_ref[:, lanes]]
        values = [jnp.concatenate([v, jnp.ones_like(v)], axis=1) for v in values]
        for first in range(0, rows, WIN):
            tile = slice(first, first + WIN)
            scores = [nt(q_ref[tile, lanes], k) for k in keys]
            top = jnp.maximum(*[jnp.max(part, axis=1, keepdims=True) for part in scores])
            both = 0.0
            for part, v in zip(scores, values):
                both = both + nn(jnp.exp(part - top).astype(BF), v)
            row_sum = both[:, DH:]
            context = both[:, :DH] / row_sum
            out_ref[tile, lanes] = context.astype(BF)
            exact_ref[tile, lanes] = context
            log_total = top + jnp.log(jnp.concatenate([row_sum, row_sum], axis=1))
            total_ref[h : h + 1, tile] = jnp.transpose(log_total)[:1]


def cross_forward(queries, own, other, earlier=()):
    rows, width = queries.shape
    keys, pairs = own.shape[0], width // 128
    tile = pl.BlockSpec((rows, 128), lambda g: (0, g))
    left = pl.BlockSpec((keys, 128), lambda g: (0, g))
    right = pl.BlockSpec((keys, 128), lambda g: (0, pairs + g))
    return run(
        "cross_forward",
        cross_forward_kernel,
        [queries, own, own, other, other],
        [tile, left, right, left, right],
        earlier,
        26,
        grid=(pairs,),
        out_specs=[tile, tile, pl.BlockSpec((None, 8, rows), lambda g: (g, 0, 0))],
        out_shape=[
            jax.ShapeDtypeStruct((rows, width), BF),
            jax.ShapeDtypeStruct((rows, width), F32),
            jax.ShapeDtypeStruct((pairs, 8, rows), F32),
        ],
        compiler_params=pltpu.CompilerParams(vmem_limit_bytes=48 * MIB),
    )


def cross_backward_kernel(
    q_ref, g_ref, exact_ref, total_ref, k0_ref, v0_ref, k1_ref, v1_ref,
    gq_ref, gk0_ref, gv0_ref, gk1_ref, gv1_ref, inner_ref, sum_ref,
):
    step, steps = pl.program_id(1), pl.num_programs(1)
    rows = q_ref.shape[0]

    @pl.when(step == 0)
    def _():
        sum_ref[...] = jnp.zeros_like(sum_ref)
        for first in range(0, rows, WIN):
            tile = slice(first, first + WIN)
            product = jnp.transpose(g_ref[tile, :].astype(F32) * exact_ref[tile, :])
            for h in range(2):
                inner_ref[h : h + 1, tile] = jnp.sum(
                    product[h * DH : (h + 1) * DH], axis=0, keepdims=True
                )

    for k_ref, v_ref, gk_ref, gv_ref in (
        (k0_ref, v0_ref, gk0_ref, gv0_ref),
        (k1_ref, v1_ref, gk1_ref, gv1_ref),
    ):
        for h in range(2):
            lanes = slice(h * DH, (h + 1) * DH)
            k, v = k_ref[:, lanes], v_ref[:, lanes]
            k_across = jnp.transpose(k)
            key_grad = jnp.zeros(k.shape, F32)
            value_grad = jnp.zeros(k.shape, F32)
            for first in range(0, rows, WIN):
                tile = slice(first, first + WIN)
                q, g = q_ref[tile, lanes], g_ref[tile, lanes]
                prob = jnp.exp(nt(k, q) - total_ref[h : h + 1, tile])
                prob_grad = nt(v, g)
                score_grad = (prob * (prob_grad - inner_ref[h : h + 1, tile])).astype(BF)
                value_grad += nn(prob.astype(BF), g)
                key_grad += nn(score_grad, q)
                sum_ref[lanes, tile] += nn(k_across, score_grad)
            gk_ref[:, lanes] = key_grad.astype(gk_ref.dtype)
            gv_ref[:, lanes] = value_grad.astype(gv_ref.dtype)

    @pl.when(step == steps - 1)
    def _():
        for first in range(0, rows, WIN):
            tile = slice(first, first + WIN)
            gq_ref[tile, :] = jnp.transpose(sum_ref[:, tile]).astype(BF)


def cross_backward(queries, grads, exact, total, own, other, earlier=()):
    rows, width = queries.shape
    keys, pairs = own.shape[0], width // 128
    parts = 4
    tile = pl.BlockSpec((rows, 128), lambda g, j: (0, g))
    left = pl.BlockSpec((keys // parts, 128), lambda g, j: (j, g))
    right = pl.BlockSpec((keys // parts, 128), lambda g, j: (j, pairs + g))
    shape = (keys, width)
    return run(
        "cross_backward",
        cross_backward_kernel,
        [queries, grads, exact, total, own, own, other, other],
        [tile, tile, tile, pl.BlockSpec((None, 8, rows), lambda g, j: (g, 0, 0))]
        + [left, right, left, right],
        earlier,
        62,
        grid=(pairs, parts),
        out_specs=[tile, left, left, left, left],
        out_shape=[
            jax.ShapeDtypeStruct(queries.shape, BF),
            jax.ShapeDtypeStruct(shape, F32),
            jax.ShapeDtypeStruct(shape, F32),
            jax.ShapeDtypeStruct(shape, BF),
            jax.ShapeDtypeStruct(shape, BF),
        ],
        scratch_shapes=[pltpu.VMEM((8, rows), F32), pltpu.VMEM((128, rows), F32)],
        compiler_params=pltpu.CompilerParams(vmem_limit_bytes=48 * MIB),
    )


def sum_keys_kernel(k0_ref, v0_ref, k1_ref, v1_ref, out_ref):
    width = k0_ref.shape[1]
    out_ref[:, :width] = (k0_ref[...] + k1_ref[...].astype(F32)).astype(BF)
    out_ref[:, width:] = (v0_ref[...] + v1_ref[...].astype(F32)).astype(BF)


def sum_keys(own, received, earlier=()):
    rows, width = own[0].shape
    tile = rows // 4
    block = pl.BlockSpec((tile, width), lambda i: (i, 0))
    return run(
        "sum_keys",
        sum_keys_kernel,
        [*own, *received],
        [block] * 4,
        earlier,
        6,
        grid=(4,),
        out_specs=pl.BlockSpec((tile, 2 * width), lambda i: (i, 0)),
        out_shape=jax.ShapeDtypeStruct((rows, 2 * width), BF),
    )


def norm_scale(stream):
    return lax.rsqrt(jnp.mean(stream * stream, axis=-1, keepdims=True) + EPSILON)


def norm_back(stream, scale, gain, incoming):
    scaled = incoming * gain
    along = jnp.mean(scaled * stream, axis=-1, keepdims=True)
    return (
        scale * scaled - stream * (scale * scale * scale) * along,
        jnp.sum(incoming * stream * scale, axis=0, keepdims=True),
    )


def gate_and_slope(u):
    inner = 0.7978845608028654 * (u + 0.044715 * u * u * u)
    bent = jnp.tanh(inner)
    half = 0.5 * (1.0 + bent)
    slope = half + 0.5 * u * (1.0 - bent * bent) * 0.7978845608028654 * (1.0 + 0.134145 * u * u)
    return u * half, slope


def row_scale(stream):
    return lax.rsqrt(jnp.mean(stream * stream, axis=-1, keepdims=True) + EPSILON)


def norm_back_kernel(count, follows, *refs):
    stream_ref, gain_ref, upper_ref = refs[:3]
    if count:
        grad_refs, weight_ref, refs = refs[3 : 3 + count], refs[3 + count], refs[4 + count :]
        incoming, first = 0.0, 0
        for grad_ref in grad_refs:
            width = grad_ref.shape[1]
            incoming = incoming + nt(grad_ref[...], weight_ref[:, first : first + width])
            first += width
    else:
        incoming, refs = refs[3][...], refs[4:]
    next_ref, refs = (refs[0], refs[1:]) if follows else (None, refs)
    stream = stream_ref[...].astype(F32)
    scale = row_scale(stream)
    scaled = incoming * gain_ref[...]
    along = jnp.mean(scaled * stream, axis=-1, keepdims=True)
    grad = upper_ref[...].astype(F32) + (scale * scaled - stream * (scale * scale * scale) * along)

    @pl.when(pl.program_id(0) == 0)
    def _():
        refs[0][...] = jnp.zeros_like(refs[0])

    refs[0][...] += jnp.sum(incoming * stream * scale, axis=0, keepdims=True)
    low = grad.astype(BF)
    if follows:
        refs[1][...] = low
        refs[2][...] = grad
        refs[3][...] = nn(low, next_ref[...]).astype(BF)
    else:
        for i, ref in enumerate(refs[1:]):

            @pl.when(pl.program_id(0) == i)
            def _(ref=ref):
                ref[...] = low


def norm_back_call(stream, gain, upper, grads, weight, following=None, earlier=()):
    rows, model = stream.shape
    count, follows = (len(grads), following is not None) if weight is not None else (0, following is not None)
    tile = pl.BlockSpec((WIN, model), lambda i: (i, 0))

    def whole(x):
        return pl.BlockSpec(x.shape, lambda i: (0, 0))

    operands = [stream, gain, upper, *grads]
    specs = [tile, whole(gain), tile] + [
        pl.BlockSpec((WIN, x.shape[1]), lambda i: (i, 0)) for x in grads
    ]
    for x in (weight, following):
        if x is not None:
            operands.append(x)
            specs.append(whole(x))
    if follows:
        outs = [(rows, kind) for kind in (BF, F32, BF)]
        out_specs = [tile] * 3
    else:
        outs = [(WIN, BF)] * (rows // WIN)
        out_specs = [pl.BlockSpec((WIN, model), lambda i: (0, 0))] * (rows // WIN)
    return run(
        "norm_back",
        functools.partial(norm_back_kernel, count, follows),
        operands,
        specs,
        earlier,
        5,
        grid=(rows // WIN,),
        out_specs=[whole(gain)] + out_specs,
        out_shape=[jax.ShapeDtypeStruct(gain.shape, F32)]
        + [jax.ShapeDtypeStruct((n, model), kind) for n, kind in outs],
        compiler_params=pltpu.CompilerParams(vmem_limit_bytes=48 * MIB),
    )


def feed_forward_kernel(
    n_ref, g_ref, x_ref, in_ref, out_ref, act_ref, pre_ref, back_ref, low_ref, high_ref, sum_ref
):
    step = pl.program_id(0)
    half = n_ref.shape[0] // 2

    @pl.when(step == 0)
    def _():
        sum_ref[...] = x_ref[...]
        back_ref[...] = jnp.zeros_like(back_ref)

    for rows in (slice(0, half), slice(half, 2 * half)):
        gate, slope = gate_and_slope(nn(n_ref[rows, :], in_ref[...]))
        activated = gate.astype(BF)
        act_ref[rows, :] = activated
        sum_ref[rows, :] += nt(activated, out_ref[...])
        pre_grad = (nn(g_ref[rows, :], out_ref[...]) * slope).astype(BF)
        pre_ref[rows, :] = pre_grad
        back_ref[rows, :] += nt(pre_grad, in_ref[...])

    @pl.when(step == pl.num_programs(0) - 1)
    def _():
        low_ref[...] = sum_ref[:half].astype(BF)
        high_ref[...] = sum_ref[half:].astype(BF)


def feed_forward(rows, grads, stream, in_weight, out_weight, earlier=()):
    count, model = rows.shape
    units, tile = in_weight.shape[1], 512
    whole = pl.BlockSpec((count, model), lambda i: (0, 0))
    half = pl.BlockSpec((count // 2, model), lambda i: (0, 0))
    weight = pl.BlockSpec((model, tile), lambda i: (0, i))
    part = pl.BlockSpec((count, tile), lambda i: (0, i))
    return run(
        "feed_forward",
        feed_forward_kernel,
        [rows, grads, stream, in_weight, out_weight],
        [whole, whole, whole, weight, weight],
        earlier,
        16,
        grid=(units // tile,),
        out_specs=[part, part, whole, half, half],
        out_shape=[jax.ShapeDtypeStruct((count, units), BF)] * 2
        + [jax.ShapeDtypeStruct((count, model), F32)]
        + [jax.ShapeDtypeStruct((count // 2, model), BF)] * 2,
        scratch_shapes=[pltpu.VMEM((count, model), F32)],
        compiler_params=pltpu.CompilerParams(vmem_limit_bytes=48 * MIB),
    )


def local(
    hidden, passages, block_ids, buckets, norm_gains, self_query, self_key, self_value, self_out,
    cross_query, cross_key, cross_value, cross_out, ffn_in, ffn_out, rel_bias, out_grad,
):
    ranks = lax.axis_size("tensor")
    rank = lax.axis_index("tensor")
    batches, rows, model = hidden.shape
    head_width = self_query.shape[1]
    width = head_width * ranks

    hw, ffn = head_width, ffn_in.shape[1]
    self_layout = [(k * hw, hw, k * width, hw) for k in range(5)]
    kv_layout = [(0, hw, 0, hw), (hw, hw, width, hw)]
    late_layout = [(0, ffn, 0, ffn), (ffn, ffn, ranks * ffn, ffn), (2 * ffn, hw, 2 * ranks * ffn, hw)]
    def option(name, *choices):
        return choices[OPT[name] % len(choices)]

    gains = gather_small(jnp.transpose(norm_gains))
    gains = jnp.transpose(gains, (1, 0, 2)).reshape(3, model).astype(F32)
    if OPT["S"] == 0:
        self_blocks = gather_ranks([self_query, self_key, self_value, self_out, cross_query])
        kv_blocks = gather_ranks([cross_key, cross_value])
    else:
        both = beside([self_query, self_key, self_value, self_out, cross_query, cross_key, cross_value])
        both = lax.all_gather(both, "tensor", axis=0)
        cut = 5 * hw
        self_blocks, kv_blocks = [both[:, :, :cut]], [both[:, :, cut:]]
    if OPT["R"] == 0:
        ids = lax.dynamic_slice_in_dim(block_ids, rank * rows, rows, 1)
        stream_low, ids, _, _ = gathered_with_ids(hidden, ids)
    else:
        ids = gathered(
            lax.dynamic_slice_in_dim(block_ids, rank * rows, rows, 1).reshape(batches, -1, WIN)
        )
        stream_low = gathered(hidden)
    encoded = gathered(passages)
    bias = window_bias(
        rel_bias,
        buckets,
        option(
            "C",
            [gains, *self_blocks, *kv_blocks],
            [gains, *self_blocks],
            [gains, *kv_blocks],
            [gains, stream_low],
            [gains, encoded],
        ),
    )
    self_pieces = gather_cores(gather_far(gather_paths(jnp.stack(self_blocks) if OPT["S"] == 0 else self_blocks[0])))
    qkv_weight, so_weight, cq_weight = gather_end(
        self_pieces,
        [self_layout[:3], [(3 * hw, hw, 0, hw)], [(4 * hw, hw, 0, hw)]],
        option("B", [bias, stream_low], [bias], [bias, encoded], []),
        OPT["S"] == 0,
    )
    late_earlier = option(
        "A", self_blocks + kv_blocks, [bias], [stream_low], [encoded], [*kv_blocks, stream_low, bias],
        self_pieces[3:4], [qkv_weight], [*self_pieces[3:4], stream_low],
    )
    if OPT["Q"] == 0:
        late_blocks = gather_ranks_at_once([ffn_in, ffn_out, cross_out], late_earlier)
    else:
        late_blocks = jnp.stack(gather_ranks([ffn_in, ffn_out, cross_out], late_earlier))
    late_paths = gather_paths(late_blocks)
    kv_pieces = gather_cores(gather_far(gather_paths(jnp.stack(kv_blocks) if OPT["S"] == 0 else kv_blocks[0])))
    (kv_weight,) = gather_end(kv_pieces, [kv_layout], option("D", [qkv_weight], [bias], [encoded]), OPT["S"] == 0)

    stream = stream_low.astype(F32)
    scale_one = norm_scale(stream)
    normed_one = (stream * scale_one * gains[0]).astype(BF)
    qkv = nn(normed_one, qkv_weight).astype(BF)
    context = self_forward(qkv, ids, bias, [kv_weight])
    after_self = stream + nt(context, so_weight)
    scale_two = norm_scale(after_self)
    normed_two = (after_self * scale_two * gains[1]).astype(BF)
    queries = nn(normed_two, cq_weight).astype(BF)

    own_kv = nn(encoded, kv_weight).astype(BF)
    other_kv = flip(own_kv, "fsdp", 1)
    late_far = gather_far(late_paths)
    incoming = gathered_after(out_grad, option("T", [qkv_weight], [context], [own_kv], late_paths[:1], late_far[3:]))
    cross_context, exact, total = cross_forward(
        queries, own_kv, other_kv, option("E", late_paths[1:], [], late_far[3:], [incoming])
    )
    late_pieces = gather_cores(late_far)
    in_weight, out_weight, co_weight = gather_end(
        late_pieces,
        [[(0, ffn, 0, ffn)], [(ffn, ffn, 0, ffn)], [(2 * ffn, hw, 0, hw)]],
        [cross_context],
        OPT["Q"] != 0,
    )

    after_cross = after_self + nt(cross_context, co_weight)
    scale_three = norm_scale(after_cross)
    normed_three = (after_cross * scale_three * gains[2]).astype(BF)
    if OPT["F"] == 0:
        activated, pre_grad, normed_grad, *output = feed_forward(
            normed_three, incoming, after_cross, in_weight, out_weight
        )
    else:
        gate, slope = gate_and_slope(nn(normed_three, in_weight))
        activated = gate.astype(BF)
        output = (after_cross + nt(activated, out_weight)).astype(BF)
        output = [output[:WIN], output[WIN:]]
        pre_grad = (nn(incoming, out_weight) * slope).astype(BF)
        normed_grad = nt(pre_grad, in_weight)
    stream_part, gain_three = norm_back(after_cross, scale_three, gains[2], normed_grad)
    grad_two = incoming.astype(F32) + stream_part
    branch_two = grad_two.astype(BF)
    context_grad = nn(branch_two, co_weight).astype(BF)
    late_grads = weight_grads(
        [normed_three, incoming, branch_two],
        [((0,), [pre_grad]), ((1,), [activated]), ((2,), [cross_context])],
        [context_grad],
    )
    late_stage = scatter_cores(late_grads)

    query_grad, key_own, value_own, key_other, value_other = cross_backward(
        queries, context_grad, exact, total, own_kv, other_kv,
        option("G", [late_grads[0], output[0]], [late_grads[0]], [output[0]]),
    )
    output = returned(output)
    kv_received = [flip(x, "fsdp", 1) for x in (key_other, value_other)]
    late_stage = scatter_paths(late_stage, [query_grad])
    if OPT["H"] == 0:
        normed_grad = nt(query_grad, cq_weight)
        stream_part, gain_two = norm_back(after_self, scale_two, gains[1], normed_grad)
        grad_one = grad_two + stream_part
        branch_one = grad_one.astype(BF)
        context_grad = nn(branch_one, so_weight).astype(BF)
    else:
        gain_two, branch_one, grad_one, context_grad = norm_back_call(
            after_self, gains[1][None], grad_two, [query_grad], cq_weight, so_weight,
            option("H", [], [], [late_stage[0]]),
        )
    kv_grad = sum_keys([key_own, value_own], kv_received, [late_stage[0]])
    encoded_grad = rows_back(kv_grad, kv_weight)
    encoded_grads = returned(encoded_grad)

    gq, gk, gv, sums = self_backward(
        qkv, context_grad, ids, bias,
        option("I", [encoded_grad[0], *late_stage[1:]], [encoded_grad[0]], [late_stage[0]], []),
    )
    late_stage = scatter_far(late_stage, [gq])
    self_grads = weight_grads(
        [normed_one, branch_one, normed_two],
        [((0,), [gq]), ((0,), [gk]), ((0,), [gv]), ((1,), [context]), ((2,), [query_grad])],
        option("J", late_stage[:1], []),
    )
    self_stage = scatter_cores(self_grads)
    kv_sums = weight_grads([encoded], [((0,), [kv_grad])], [self_grads[0]])
    kv_stage = scatter_cores(kv_sums)
    if OPT["K"] == 0:
        late_blocks = scatter_end(late_stage, late_layout, [kv_sums[0]])
        self_stage = scatter_paths(self_stage, [late_blocks])
    else:
        self_stage = scatter_paths(self_stage, [kv_sums[0]])
        late_blocks = scatter_end(late_stage, late_layout, [self_stage[0]])
    kv_stage = scatter_paths(kv_stage, [self_stage[0], late_blocks])
    late_total = scatter_tensor(late_blocks)
    in_total, out_total, co_total = late_total[:, :ffn], late_total[:, ffn : 2 * ffn], late_total[:, 2 * ffn :]
    if OPT["L"] == 0:
        gain_one, *input_grad = norm_back_call(
            stream_low, gains[0][None], grad_one, [gq, gk, gv], qkv_weight, None, [self_stage[0]]
        )
    elif OPT["L"] == 1:
        gain_one, *input_grad = norm_back_call(
            stream_low, gains[0][None], grad_one, [gq, gk, gv], qkv_weight, None, [kv_stage[0]]
        )
    else:
        normed_grad = sum(
            nt(x, qkv_weight[:, k * width : (k + 1) * width]) for k, x in enumerate((gq, gk, gv))
        )
        stream_part, gain_one = norm_back(stream, scale_one, gains[0], normed_grad)
        input_grad = (grad_one + stream_part).astype(BF)
        input_grad = [input_grad[:WIN], input_grad[WIN:]]
    input_grads = returned(input_grad)
    bias_lanes = bucket_sums(
        sums, buckets, rel_bias.shape[0], option("M", [kv_stage[0]], [self_stage[0]], [self_stage[0], input_grad[0]])
    )
    self_stage = scatter_far(self_stage, option("N", [bias_lanes], [kv_stage[0]], [input_grad[0]]))
    kv_stage = scatter_far(kv_stage, [self_stage[0]])
    self_total = scatter_tensor(scatter_end(self_stage, self_layout, option("P", [kv_stage[0]], [])))
    q_total, k_total, v_total, so_total, cq_total = column_blocks(self_total, 5)
    kv_total = scatter_tensor(scatter_end(kv_stage, kv_layout, [kv_stage[0]]))

    bias_own = jnp.transpose(jnp.sum(bias_lanes, axis=2))
    small = jnp.concatenate(
        [gain_one.reshape(-1), gain_two.reshape(-1), gain_three.reshape(-1), bias_own.reshape(-1)]
    )
    pad = -small.shape[0] % 1024
    small = jnp.pad(small, (0, pad)).reshape(8, -1)
    small = sum_everywhere(small).reshape(-1)
    gains_sum = jnp.transpose(small[: 3 * model].reshape(3, model))
    bias_total = small[3 * model : 3 * model + rel_bias.size].reshape(rel_bias.shape)

    return (
        by_batch(output, BF),
        by_batch(input_grads, F32),
        by_batch(encoded_grads, F32),
        gains_sum,
        q_total,
        k_total,
        v_total,
        so_total,
        cq_total,
        kv_total[:, :head_width],
        kv_total[:, head_width:],
        co_total,
        in_total,
        out_total,
        bias_total,
    )


def solution(mesh):
    rows = P(None, ("fsdp", "tensor"), None)
    weight = P("fsdp", "tensor")
    in_specs = (rows, rows, P(None, "fsdp"), P(), P("fsdp", None)) + (weight,) * 10 + (P(), rows)
    out_specs = (rows, rows, rows, P()) + (weight,) * 10 + (P(),)
    return jax.shard_map(local, mesh=mesh, in_specs=in_specs, out_specs=out_specs, check_vma=False)
```

```python
import functools

import jax
import jax.numpy as jnp
from jax import lax
from jax.experimental import pallas as pl
from jax.experimental.pallas import tpu as pltpu
from jax.sharding import PartitionSpec as P

DH = 64
WIN = 256
EPSILON = 1e-06
MASKED = -1000000000.0
BF = jnp.bfloat16
F32 = jnp.float32
MIB = 1024 * 1024
TOOK = {'assemble': 3, 'self_forward': 1, 'self_backward': 1, 'weight_grads': 0.5, 'sum_keys': 1, 'rows_back': 1, 'sum_far': 1, 'spread': 1, 'pick_with_ids': 1, 'pick': 1, 'join': 1, 'window_bias': 1, 'cross_forward': 1, 'cross_backward': 1, 'bucket_sums': 1, 'sum_cores': 1, 'sum_paths': 2, 'feed_forward': 1, 'norm_back': 1, 'stack': 1, 'project': 1}
OPT = {'T': 0, 'Q': 1, 'R': 0, 'S': 0, 'A': 0, 'B': 1, 'C': 0, 'D': 1, 'E': 0, 'F': 1, 'G': 0, 'H': 0, 'I': 0, 'J': 0, 'K': 1, 'L': 2, 'M': 0, 'N': 0, 'P': 1}


def nn(left, right):
    return jnp.dot(left, right, preferred_element_type=F32)


def nt(left, right):
    return lax.dot_general(left, right, (((1,), (1,)), ((), ())), preferred_element_type=F32)


def tn(left, right):
    return lax.dot_general(left, right, (((0,), (0,)), ((), ())), preferred_element_type=F32)


def shift(x, axis, by):
    size = lax.axis_size(axis)
    if by % size == 0:
        return x
    return lax.ppermute(x, axis, [(i, (i + by) % size) for i in range(size)])


def flip(x, axis, bits):
    size = lax.axis_size(axis)
    return lax.ppermute(x, axis, [(i, i ^ bits) for i in range(size)])


def two_way(x, swapped):
    first, second = (4, 2) if swapped else (2, 4)
    return lax.ppermute(x, "fsdp", [(i, i ^ (second if i & 1 else first)) for i in range(8)])


def assemble_kernel(starts, by_distance, *refs):
    pieces, outs = refs[:8], refs[8:]
    me = lax.axis_index("fsdp")
    odd = lax.rem(me, 2)
    x_bit, y_bit = lax.rem(me // 2, 2), me // 4

    def flipped(dx, dy, dc):
        new_x = x_bit + dx - 2 * x_bit * dx
        new_y = y_bit + dy - 2 * y_bit * dy
        new_c = odd + dc - 2 * odd * dc
        return new_y * 4 + new_x * 2 + new_c

    even = 1 - odd
    places = [
        flipped(0, 0, 0),
        flipped(even, odd, 0),
        flipped(odd, even, 0),
        flipped(1, 1, 0),
        flipped(0, 0, 1),
        flipped(odd, even, 1),
        flipped(even, odd, 1),
        flipped(1, 1, 1),
    ]
    ranks, rows = pieces[0].shape[0], pieces[0].shape[1]
    rank = lax.axis_index("tensor")
    for place, piece in zip(places, pieces):
        here = pl.ds(pl.multiple_of(place * rows, rows), rows)
        for s in range(ranks):
            block = piece[lax.rem(rank - s + ranks, ranks) if by_distance else s]
            for out_ref, parts in zip(outs, starts):
                for first, width, base, stride in parts:
                    out_ref[here, base + s * stride : base + s * stride + width] = block[
                        :, first : first + width
                    ]


def gather_paths(piece):
    if lax.axis_size("fsdp") != 8 or piece.shape[1] % 16:
        return [piece]
    return [piece, two_way(piece, False), two_way(piece, True)]


def gather_far(pieces):
    if len(pieces) == 1:
        return pieces
    return pieces + [two_way(pieces[1], True)]


def gather_cores(pieces):
    if len(pieces) == 1:
        return [lax.all_gather(pieces[0], "fsdp", axis=1, tiled=True)]
    return pieces + [flip(p, "fsdp", 1) for p in pieces]


def gather_end(pieces, layout, earlier=(), by_distance=True):
    ranks, rows = pieces[0].shape[:2]
    widths = [sum(part[1] for part in parts) * ranks for parts in layout]
    if len(pieces) == 1:
        outs = []
        rank = lax.axis_index("tensor")
        order = lax.rem(rank + ranks - jnp.arange(ranks, dtype=jnp.int32), ranks)
        blocks = jnp.take(pieces[0], order, axis=0) if by_distance else pieces[0]
        for parts in layout:
            columns = {}
            for first, width, base, stride in parts:
                for s in range(ranks):
                    columns[base + s * stride] = blocks[s, :, first : first + width]
            outs.append(jnp.concatenate([columns[k] for k in sorted(columns)], axis=1))
        return outs
    return run(
        "assemble",
        functools.partial(assemble_kernel, layout, by_distance),
        pieces,
        [pl.BlockSpec(memory_space=pltpu.VMEM)] * 8,
        earlier,
        sum(widths) * rows / 96000 + 1,
        out_shape=[jax.ShapeDtypeStruct((8 * rows, w), pieces[0].dtype) for w in widths],
        compiler_params=pltpu.CompilerParams(vmem_limit_bytes=48 * MIB),
    )


def run(name, kernel, operands, in_specs, earlier=(), took=1, **how):
    count, took = len(earlier), took * TOOK[name]

    def body(*refs):
        kernel(*refs[count:])

    return pl.pallas_call(
        body,
        in_specs=[pl.BlockSpec(memory_space=pl.ANY)] * count + in_specs,
        cost_estimate=pl.CostEstimate(
            flops=int(took * 1.1e9), bytes_accessed=int(took * 3.5e6), transcendentals=0
        ),
        name=name,
        **how,
    )(*earlier, *operands)


def join_kernel(*refs):
    first = 0
    for ref in refs[:-1]:
        refs[-1][:, first : first + ref.shape[1]] = ref[...]
        first += ref.shape[1]


def joined(parts, earlier=()):
    if parts[0].shape[0] % 16:
        return beside(parts)
    return run(
        "join",
        join_kernel,
        parts,
        [pl.BlockSpec(memory_space=pltpu.VMEM)] * len(parts),
        earlier,
        1.5,
        out_shape=jax.ShapeDtypeStruct(
            (parts[0].shape[0], sum(x.shape[1] for x in parts)), parts[0].dtype
        ),
    )


def spread_kernel(*refs):
    out_ref, first = refs[-1], 0
    for ref in refs[:-1]:
        for s in range(out_ref.shape[0]):
            out_ref[s, :, first : first + ref.shape[1]] = ref[...]
        first += ref.shape[1]


def gather_ranks_at_once(shards, earlier=()):
    ranks, rows = lax.axis_size("tensor"), shards[0].shape[0]
    width = sum(x.shape[1] for x in shards)
    if rows % 16:
        return lax.all_gather(beside(shards), "tensor", axis=0)
    copies = run(
        "spread",
        spread_kernel,
        shards,
        [pl.BlockSpec(memory_space=pltpu.VMEM)] * len(shards),
        earlier,
        out_shape=jax.ShapeDtypeStruct((ranks, rows, width), shards[0].dtype),
    )
    return lax.all_to_all(copies, "tensor", split_axis=0, concat_axis=0, tiled=True)


def gather_ranks(shards, earlier=()):
    own = joined(shards, earlier)
    return [shift(own, "tensor", s) for s in range(lax.axis_size("tensor"))]


def gather_small(shard):
    size = lax.axis_size("fsdp")
    held = shard[None]
    bit = 1
    while bit < size:
        held = jnp.concatenate([held, flip(held, "fsdp", bit)], axis=0)
        bit *= 2
    order = jnp.bitwise_xor(jnp.arange(size, dtype=jnp.int32), lax.axis_index("fsdp"))
    return jnp.take(held, order, axis=0)


def sum_everywhere(x):
    for axis in ("fsdp", "tensor"):
        bits = []
        while 1 << len(bits) < lax.axis_size(axis):
            bits.append(1 << len(bits))
        if len(bits) % 2:
            x = x + flip(x, axis, bits.pop(0))
        for one, two in zip(bits[::2], bits[1::2]):
            x = (x + flip(x, axis, one)) + (flip(x, axis, two) + flip(x, axis, one + two))
    return x


def grad_kernel(phases, left_count, *refs):
    lefts, refs = refs[:left_count], refs[left_count:]
    outs, across_ref, rows_ref = refs[-4:-2], refs[-2], refs[-1]
    step = pl.program_id(0)
    me = lax.axis_index("fsdp")
    odd = lax.rem(me, 2)
    x_bit, y_bit = lax.rem(me // 2, 2), me // 4
    first, ref, before = 0, 0, None
    for indices, count, blocks in phases:
        rights = refs[ref : ref + count]
        ref += count

        if indices != before:

            @pl.when(step == first)
            def _(indices=indices):
                done = 0
                for i in indices:
                    across_ref[:, done : done + lefts[i].shape[0]] = jnp.transpose(lefts[i][...])
                    done += lefts[i].shape[0]

        before = indices

        @pl.when((step >= first) & (step < first + blocks))
        def _(rights=rights):
            total, done = 0.0, 0
            for right in rights:
                total = total + nn(across_ref[:, done : done + right.shape[0]], right[...])
                done += right.shape[0]
            rows_ref[...] = total.astype(BF)

        first += blocks
    size = rows_ref.shape[0] // 8
    for out_ref, core in zip(outs, (odd, 1 - odd)):
        even = 1 - core
        for place, (dx, dy) in enumerate(((0, 0), (core, even), (even, core), (1, 1))):
            block = (y_bit + dy - 2 * y_bit * dy) * 4 + (x_bit + dx - 2 * x_bit * dx) * 2 + core
            out_ref[place * size : (place + 1) * size, :] = rows_ref[
                pl.ds(pl.multiple_of(block * size, size), size), :
            ]


def weight_grads(lefts, phases, earlier=(), tile=768):
    model = lefts[0].shape[1]
    if lax.axis_size("fsdp") != 8:
        whole = []
        for indices, rights in phases:
            rights = [beside(list(y)) if y.ndim == 3 else y for y in rights]
            whole.append(tn(below([lefts[i] for i in indices]), below(rights)))
        return [beside(whole).astype(BF)]
    specs = [pl.BlockSpec(x.shape, lambda i: (0, 0)) for x in lefts]
    operands, sizes, first = list(lefts), [], 0
    for indices, rights in phases:
        deep = rights[0].ndim == 3
        count = rights[0].shape[0] if deep else rights[0].shape[1] // tile
        operands += rights
        for y in rights:
            if deep:
                shape, where = (None, y.shape[1], tile), lambda i, k: (k, 0, 0)
            else:
                shape, where = (y.shape[0], tile), lambda i, k: (0, k)
            specs.append(
                pl.BlockSpec(
                    shape,
                    lambda i, f=first, n=count, where=where: where(i, jnp.clip(i - f, 0, n - 1)),
                )
            )
        sizes.append((indices, len(rights), count))
        first += count
    deepest = max(sum(lefts[i].shape[0] for i in indices) for indices, _ in phases)
    shape = jax.ShapeDtypeStruct((model // 2, first * tile), BF)
    kept_and_sent = run(
        "weight_grads",
        functools.partial(grad_kernel, sizes, len(lefts)),
        [*operands],
        specs,
        earlier,
        first * 1.4,
        grid=(first,),
        out_specs=[pl.BlockSpec((model // 2, tile), lambda i: (0, i))] * 2,
        out_shape=[shape, shape],
        scratch_shapes=[pltpu.VMEM((model, deepest), BF), pltpu.VMEM((model, tile), BF)],
        compiler_params=pltpu.CompilerParams(vmem_limit_bytes=48 * MIB),
    )
    return list(kept_and_sent)


def rows_back_kernel(grad_ref, weight_ref, low_ref, high_ref):
    half = low_ref.shape[0]
    low_ref[...] = nt(grad_ref[:half], weight_ref[...]).astype(BF)
    high_ref[...] = nt(grad_ref[half:], weight_ref[...]).astype(BF)


def rows_back(grad, weight, earlier=()):
    rows, model = grad.shape[0], weight.shape[0]
    tile = 256
    return run(
        "rows_back",
        rows_back_kernel,
        [grad, weight],
        [
            pl.BlockSpec(grad.shape, lambda i: (0, 0)),
            pl.BlockSpec((tile, weight.shape[1]), lambda i: (i, 0)),
        ],
        earlier,
        6,
        grid=(model // tile,),
        out_specs=[pl.BlockSpec((rows // 2, tile), lambda i: (0, i))] * 2,
        out_shape=[jax.ShapeDtypeStruct((rows // 2, model), BF)] * 2,
        compiler_params=pltpu.CompilerParams(vmem_limit_bytes=48 * MIB),
    )


def scatter_cores(grads):
    if len(grads) == 1:
        return [lax.psum_scatter(grads[0].astype(F32), "fsdp", scatter_dimension=0, tiled=True)]
    return [grads[0], flip(grads[1], "fsdp", 1)]


def halves_kernel(kept_ref, sent_ref, low_ref, high_ref):
    half = low_ref.shape[0]
    for out_ref, rows in ((low_ref, slice(0, half)), (high_ref, slice(half, 2 * half))):
        both = kept_ref[rows, :].astype(F32) + sent_ref[rows, :].astype(F32)
        out_ref[...] = both.astype(out_ref.dtype)


def sum_halves(name, kept, received, low_type, earlier):
    rows, width = kept.shape
    tile = 768
    whole = pl.BlockSpec((rows, tile), lambda i: (0, i))
    half = pl.BlockSpec((rows // 2, tile), lambda i: (0, i))
    return run(
        name,
        halves_kernel,
        [kept, received],
        [whole, whole],
        earlier,
        rows * width / 300000,
        grid=(width // tile,),
        out_specs=[half, half],
        out_shape=[
            jax.ShapeDtypeStruct((rows // 2, width), low_type),
            jax.ShapeDtypeStruct((rows // 2, width), BF),
        ],
        compiler_params=pltpu.CompilerParams(vmem_limit_bytes=48 * MIB),
    )


def scatter_paths(stage, earlier=()):
    if len(stage) == 1:
        return stage
    low, high = sum_halves("sum_cores", *stage, BF, earlier)
    return [low, two_way(high, False)]


def scatter_far(stage, earlier=()):
    if len(stage) == 1:
        return stage
    low, high = sum_halves("sum_paths", *stage, F32, earlier)
    return [low, two_way(high, True)]


def blocks_kernel(layout, kept_ref, received_ref, out_ref):
    total = (kept_ref[...] + received_ref[...].astype(F32)).astype(BF)
    for s in range(out_ref.shape[0]):
        for first, width, base, stride in layout:
            out_ref[s, :, first : first + width] = total[
                :, base + s * stride : base + s * stride + width
            ]


def scatter_end(stage, layout, earlier=()):
    ranks = lax.axis_size("tensor")
    if len(stage) == 1:
        parts = [
            jnp.concatenate(
                [stage[0][:, b + s * d : b + s * d + w] for _, w, b, d in layout], axis=1
            )
            for s in range(ranks)
        ]
        return jnp.stack(parts).astype(BF)
    rows, width = stage[0].shape
    return run(
        "sum_far",
        functools.partial(blocks_kernel, layout),
        stage,
        [pl.BlockSpec(memory_space=pltpu.VMEM)] * 2,
        earlier,
        2,
        out_shape=jax.ShapeDtypeStruct((ranks, rows, width // ranks), BF),
        compiler_params=pltpu.CompilerParams(vmem_limit_bytes=48 * MIB),
    )


def scatter_tensor(blocks):
    parts = lax.all_to_all(blocks, "tensor", split_axis=0, concat_axis=0, tiled=True)
    return jnp.sum(parts.astype(F32), axis=0)


def column_blocks(x, count):
    width = x.shape[1] // count
    return [x[:, s * width : (s + 1) * width] for s in range(count)]


def round_moves(r, back):
    size, ranks = lax.axis_size("fsdp"), lax.axis_size("tensor")
    pairs = []
    for f in range(size):
        for t in range(ranks):
            c, t1, t0 = f & 1, t >> 1, t & 1
            pair = (f * ranks + t, ((f ^ c) | t0) * ranks + 2 * (r ^ t1) + c)
            pairs.append(pair[::-1] if back else pair)
    return pairs


def pick_with_ids_kernel(x_ref, ids_ref, *outs):
    high = lax.axis_index("tensor") // 2
    rows = x_ref.shape[1]
    for r, out_ref in enumerate(outs):
        b = high + r - 2 * high * r
        out_ref[:rows] = x_ref[b]
        out_ref[rows:] = jnp.zeros((out_ref.shape[0] - rows, x_ref.shape[2]), BF)
        for w in range(rows // WIN):
            place = lax.rem(ids_ref[b, w], WIN).astype(F32).astype(BF)
            out_ref[rows + 16 * w : rows + 16 * (w + 1), :WIN] = jnp.broadcast_to(place, (16, WIN))


def gathered_with_ids(x, ids, earlier=()):
    rows, width = x.shape[1:]
    windows = rows // WIN
    parts = run(
        "pick_with_ids",
        pick_with_ids_kernel,
        [x, ids.reshape(ids.shape[0], windows, 1, WIN)],
        [pl.BlockSpec(memory_space=pltpu.VMEM)] * 2,
        earlier,
        out_shape=[jax.ShapeDtypeStruct((rows + 16 * windows, width), BF)] * 2,
    )
    moved = [lax.ppermute(y, ("fsdp", "tensor"), round_moves(r, False)) for r, y in enumerate(parts)]
    places = [y[rows + 16 * w : rows + 16 * w + 1, :WIN] for y in moved for w in range(windows)]
    return below([y[:rows] for y in moved]), below(places).astype(jnp.int32), moved, parts[:1]


def gathered(x):
    high = lax.axis_index("tensor") // 2
    parts = [
        lax.ppermute(
            lax.dynamic_index_in_dim(x, r ^ high, 0, keepdims=False),
            ("fsdp", "tensor"),
            round_moves(r, False),
        )
        for r in range(2)
    ]
    return below(parts)


def pick_kernel(x_ref, *outs):
    high = lax.axis_index("tensor") // 2
    for r, out_ref in enumerate(outs):
        out_ref[...] = x_ref[high + r - 2 * high * r]


def pick_with_ids_kernel(x_ref, ids_ref, *outs):
    high = lax.axis_index("tensor") // 2
    rows = x_ref.shape[1]
    for r, out_ref in enumerate(outs):
        b = high + r - 2 * high * r
        out_ref[:rows] = x_ref[b]
        out_ref[rows:] = jnp.zeros((out_ref.shape[0] - rows, x_ref.shape[2]), BF)
        for w in range(rows // WIN):
            place = lax.rem(ids_ref[b, w], WIN).astype(F32).astype(BF)
            out_ref[rows + 16 * w : rows + 16 * (w + 1), :WIN] = jnp.broadcast_to(place, (16, WIN))


def gathered_with_ids(x, ids, earlier=()):
    rows, width = x.shape[1:]
    windows = rows // WIN
    parts = run(
        "pick_with_ids",
        pick_with_ids_kernel,
        [x, ids.reshape(ids.shape[0], windows, 1, WIN)],
        [pl.BlockSpec(memory_space=pltpu.VMEM)] * 2,
        earlier,
        out_shape=[jax.ShapeDtypeStruct((rows + 16 * windows, width), BF)] * 2,
    )
    moved = [lax.ppermute(y, ("fsdp", "tensor"), round_moves(r, False)) for r, y in enumerate(parts)]
    places = [y[rows + 16 * w : rows + 16 * w + 1, :WIN] for y in moved for w in range(windows)]
    return below([y[:rows] for y in moved]), below(places).astype(jnp.int32), moved, parts[:1]


def gathered_after(x, earlier):
    parts = run(
        "pick",
        pick_kernel,
        [x],
        [pl.BlockSpec(memory_space=pltpu.VMEM)],
        earlier,
        out_shape=[jax.ShapeDtypeStruct(x.shape[1:], x.dtype)] * 2,
        compiler_params=pltpu.CompilerParams(vmem_limit_bytes=48 * MIB),
    )
    moved = [lax.ppermute(y, ("fsdp", "tensor"), round_moves(r, False)) for r, y in enumerate(parts)]
    return below(moved)


def returned(parts):
    return [
        lax.ppermute(x, ("fsdp", "tensor"), round_moves(r, True)) for r, x in enumerate(parts)
    ]


def by_batch(parts, dtype):
    high = lax.axis_index("tensor") // 2
    return jnp.stack([jnp.where(high == r, parts[0], parts[1]) for r in range(2)]).astype(dtype)


def beside(blocks):
    return jnp.concatenate(list(blocks), axis=1)


def below(blocks):
    return jnp.concatenate(list(blocks), axis=0)


def bias_kernel(heads, table_ref, bucket_ref, out_ref):
    group = pl.program_id(0)
    count = out_ref.shape[0]
    buckets = table_ref.shape[0]

    def some_rows(i, carry):
        rows = pl.ds(i * 32, 32)
        bucket = bucket_ref[rows, :]
        found = [jnp.zeros(bucket.shape, F32) for _ in range(count)]
        for b in range(buckets):
            here = bucket == b
            for h in range(count):
                found[h] = jnp.where(here, table_ref[b, group * count + h], found[h])
        for h in range(count):
            out_ref[h, rows, :] = found[h]
        return carry

    lax.fori_loop(0, bucket_ref.shape[0] // 32, some_rows, 0)


def window_bias(table, buckets, earlier=()):
    heads = table.shape[1]
    count = 4
    return run(
        "window_bias",
        functools.partial(bias_kernel, heads),
        [table, buckets],
        [
            pl.BlockSpec(memory_space=pltpu.SMEM),
            pl.BlockSpec((WIN, WIN), lambda g: (0, 0)),
        ],
        earlier,
        9,
        grid=(heads // count,),
        out_specs=pl.BlockSpec((count, WIN, WIN), lambda g: (g, 0, 0)),
        out_shape=jax.ShapeDtypeStruct((heads, WIN, WIN), F32),
    )


def allowed_pairs(col_ref, row_ref, window):
    rows = lax.broadcasted_iota(jnp.int32, (WIN, WIN), 0)
    cols = lax.broadcasted_iota(jnp.int32, (WIN, WIN), 1)
    return (col_ref[window] == row_ref[window]) & (cols <= rows)


def self_softmax(q, k, bias, allowed):
    scores = jnp.where(allowed, nt(q, k) + bias, MASKED)
    raised = jnp.exp(scores - jnp.max(scores, axis=1, keepdims=True))
    return raised / jnp.sum(raised, axis=1, keepdims=True)


def self_forward_kernel(q_ref, k_ref, v_ref, col_ref, row_ref, bias_ref, out_ref):
    for w in range(q_ref.shape[0] // WIN):
        allowed = allowed_pairs(col_ref, row_ref, w)
        rows = slice(w * WIN, (w + 1) * WIN)
        for h in range(2):
            lanes = slice(h * DH, (h + 1) * DH)
            prob = self_softmax(q_ref[rows, lanes], k_ref[rows, lanes], bias_ref[h], allowed)
            out_ref[rows, lanes] = nn(prob.astype(BF), v_ref[rows, lanes]).astype(BF)


def self_forward(qkv, ids, bias, earlier=()):
    rows, width = qkv.shape[0], qkv.shape[1] // 3
    pairs, windows = width // 128, rows // WIN

    def part(k):
        return pl.BlockSpec((rows, 128), lambda g, k=k: (0, k * pairs + g))

    return run(
        "self_forward",
        self_forward_kernel,
        [qkv, qkv, qkv, ids.reshape(windows, WIN, 1), ids.reshape(windows, 1, WIN), bias],
        [
            part(0),
            part(1),
            part(2),
            pl.BlockSpec((windows, WIN, 1), lambda g: (0, 0, 0)),
            pl.BlockSpec((windows, 1, WIN), lambda g: (0, 0, 0)),
            pl.BlockSpec((2, WIN, WIN), lambda g: (g, 0, 0)),
        ],
        earlier,
        12,
        grid=(pairs,),
        out_specs=part(0),
        out_shape=jax.ShapeDtypeStruct((rows, width), BF),
    )


def self_backward_kernel(
    q_ref, k_ref, v_ref, g_ref, col_ref, row_ref, bias_ref, gq_ref, gk_ref, gv_ref, sum_ref
):
    for w in range(q_ref.shape[0] // WIN):
        allowed = allowed_pairs(col_ref, row_ref, w)
        rows = slice(w * WIN, (w + 1) * WIN)
        for h in range(2):
            lanes = slice(h * DH, (h + 1) * DH)
            q, k, v = q_ref[rows, lanes], k_ref[rows, lanes], v_ref[rows, lanes]
            g = g_ref[rows, lanes]
            prob = self_softmax(q, k, bias_ref[h], allowed)
            prob_grad = nt(g, v)
            inner = jnp.sum(prob_grad * prob, axis=1, keepdims=True)
            score_grad = (prob * (prob_grad - inner)).astype(BF)
            gq_ref[rows, lanes] = nn(score_grad, k).astype(BF)
            gk_ref[rows, lanes] = tn(score_grad, q).astype(BF)
            gv_ref[rows, lanes] = tn(prob.astype(BF), g).astype(BF)
            if w:
                sum_ref[h] += score_grad.astype(F32)
            else:
                sum_ref[h] = score_grad.astype(F32)


def self_backward(qkv, grad, ids, bias, earlier=()):
    rows, width = qkv.shape[0], qkv.shape[1] // 3
    pairs, windows = width // 128, rows // WIN

    def part(k):
        return pl.BlockSpec((rows, 128), lambda g, k=k: (0, k * pairs + g))

    tables = pl.BlockSpec((2, WIN, WIN), lambda g: (g, 0, 0))
    return run(
        "self_backward",
        self_backward_kernel,
        [qkv, qkv, qkv, grad, ids.reshape(windows, WIN, 1), ids.reshape(windows, 1, WIN), bias],
        [
            part(0),
            part(1),
            part(2),
            part(0),
            pl.BlockSpec((windows, WIN, 1), lambda g: (0, 0, 0)),
            pl.BlockSpec((windows, 1, WIN), lambda g: (0, 0, 0)),
            tables,
        ],
        earlier,
        18,
        grid=(pairs,),
        out_specs=[part(0)] * 3 + [tables],
        out_shape=[jax.ShapeDtypeStruct((rows, width), BF)] * 3
        + [jax.ShapeDtypeStruct((2 * pairs, WIN, WIN), F32)],
    )


def bucket_kernel(sum_ref, bucket_ref, out_ref):
    def one_bucket(b, carry):
        here = bucket_ref[...] == b
        for h in range(sum_ref.shape[0]):
            out_ref[h, pl.ds(b, 1), :] = jnp.sum(
                jnp.where(here, sum_ref[h], 0.0), axis=0, keepdims=True
            )
        return carry

    lax.fori_loop(0, out_ref.shape[1], one_bucket, 0)


def bucket_sums(sums, buckets, count, earlier=()):
    heads = sums.shape[0]
    return run(
        "bucket_sums",
        bucket_kernel,
        [sums, buckets],
        [
            pl.BlockSpec((4, WIN, WIN), lambda g: (g, 0, 0)),
            pl.BlockSpec((WIN, WIN), lambda g: (0, 0)),
        ],
        earlier,
        13,
        grid=(heads // 4,),
        out_specs=pl.BlockSpec((4, count, WIN), lambda g: (g, 0, 0)),
        out_shape=jax.ShapeDtypeStruct((heads, count, WIN), F32),
    )


def cross_forward_kernel(q_ref, k0_ref, v0_ref, k1_ref, v1_ref, out_ref, exact_ref, total_ref):
    rows = q_ref.shape[0]
    for h in range(2):
        lanes = slice(h * DH, (h + 1) * DH)
        keys = [k0_ref[:, lanes], k1_ref[:, lanes]]
        values = [v0_ref[:, lanes], v1_ref[:, lanes]]
        values = [jnp.concatenate([v, jnp.ones_like(v)], axis=1) for v in values]
        for first in range(0, rows, WIN):
            tile = slice(first, first + WIN)
            scores = [nt(q_ref[tile, lanes], k) for k in keys]
            top = jnp.maximum(*[jnp.max(part, axis=1, keepdims=True) for part in scores])
            both = 0.0
            for part, v in zip(scores, values):
                both = both + nn(jnp.exp(part - top).astype(BF), v)
            row_sum = both[:, DH:]
            context = both[:, :DH] / row_sum
            out_ref[tile, lanes] = context.astype(BF)
            exact_ref[tile, lanes] = context
            log_total = top + jnp.log(jnp.concatenate([row_sum, row_sum], axis=1))
            total_ref[h : h + 1, tile] = jnp.transpose(log_total)[:1]


def cross_forward(queries, own, other, earlier=()):
    rows, width = queries.shape
    keys, pairs = own.shape[0], width // 128
    tile = pl.BlockSpec((rows, 128), lambda g: (0, g))
    left = pl.BlockSpec((keys, 128), lambda g: (0, g))
    right = pl.BlockSpec((keys, 128), lambda g: (0, pairs + g))
    return run(
        "cross_forward",
        cross_forward_kernel,
        [queries, own, own, other, other],
        [tile, left, right, left, right],
        earlier,
        26,
        grid=(pairs,),
        out_specs=[tile, tile, pl.BlockSpec((None, 8, rows), lambda g: (g, 0, 0))],
        out_shape=[
            jax.ShapeDtypeStruct((rows, width), BF),
            jax.ShapeDtypeStruct((rows, width), F32),
            jax.ShapeDtypeStruct((pairs, 8, rows), F32),
        ],
        compiler_params=pltpu.CompilerParams(vmem_limit_bytes=48 * MIB),
    )


def cross_backward_kernel(
    q_ref, g_ref, exact_ref, total_ref, k0_ref, v0_ref, k1_ref, v1_ref,
    gq_ref, gk0_ref, gv0_ref, gk1_ref, gv1_ref, inner_ref, sum_ref,
):
    step, steps = pl.program_id(1), pl.num_programs(1)
    rows = q_ref.shape[0]

    @pl.when(step == 0)
    def _():
        sum_ref[...] = jnp.zeros_like(sum_ref)
        for first in range(0, rows, WIN):
            tile = slice(first, first + WIN)
            product = jnp.transpose(g_ref[tile, :].astype(F32) * exact_ref[tile, :])
            for h in range(2):
                inner_ref[h : h + 1, tile] = jnp.sum(
                    product[h * DH : (h + 1) * DH], axis=0, keepdims=True
                )

    for k_ref, v_ref, gk_ref, gv_ref in (
        (k0_ref, v0_ref, gk0_ref, gv0_ref),
        (k1_ref, v1_ref, gk1_ref, gv1_ref),
    ):
        for h in range(2):
            lanes = slice(h * DH, (h + 1) * DH)
            k, v = k_ref[:, lanes], v_ref[:, lanes]
            k_across = jnp.transpose(k)
            key_grad = jnp.zeros(k.shape, F32)
            value_grad = jnp.zeros(k.shape, F32)
            for first in range(0, rows, WIN):
                tile = slice(first, first + WIN)
                q, g = q_ref[tile, lanes], g_ref[tile, lanes]
                prob = jnp.exp(nt(k, q) - total_ref[h : h + 1, tile])
                prob_grad = nt(v, g)
                score_grad = (prob * (prob_grad - inner_ref[h : h + 1, tile])).astype(BF)
                value_grad += nn(prob.astype(BF), g)
                key_grad += nn(score_grad, q)
                sum_ref[lanes, tile] += nn(k_across, score_grad)
            gk_ref[:, lanes] = key_grad.astype(gk_ref.dtype)
            gv_ref[:, lanes] = value_grad.astype(gv_ref.dtype)

    @pl.when(step == steps - 1)
    def _():
        for first in range(0, rows, WIN):
            tile = slice(first, first + WIN)
            gq_ref[tile, :] = jnp.transpose(sum_ref[:, tile]).astype(BF)


def cross_backward(queries, grads, exact, total, own, other, earlier=()):
    rows, width = queries.shape
    keys, pairs = own.shape[0], width // 128
    parts = 4
    tile = pl.BlockSpec((rows, 128), lambda g, j: (0, g))
    left = pl.BlockSpec((keys // parts, 128), lambda g, j: (j, g))
    right = pl.BlockSpec((keys // parts, 128), lambda g, j: (j, pairs + g))
    shape = (keys, width)
    return run(
        "cross_backward",
        cross_backward_kernel,
        [queries, grads, exact, total, own, own, other, other],
        [tile, tile, tile, pl.BlockSpec((None, 8, rows), lambda g, j: (g, 0, 0))]
        + [left, right, left, right],
        earlier,
        62,
        grid=(pairs, parts),
        out_specs=[tile, left, left, left, left],
        out_shape=[
            jax.ShapeDtypeStruct(queries.shape, BF),
            jax.ShapeDtypeStruct(shape, F32),
            jax.ShapeDtypeStruct(shape, F32),
            jax.ShapeDtypeStruct(shape, BF),
            jax.ShapeDtypeStruct(shape, BF),
        ],
        scratch_shapes=[pltpu.VMEM((8, rows), F32), pltpu.VMEM((128, rows), F32)],
        compiler_params=pltpu.CompilerParams(vmem_limit_bytes=48 * MIB),
    )


def sum_keys_kernel(k0_ref, v0_ref, k1_ref, v1_ref, out_ref):
    width = k0_ref.shape[1]
    out_ref[:, :width] = (k0_ref[...] + k1_ref[...].astype(F32)).astype(BF)
    out_ref[:, width:] = (v0_ref[...] + v1_ref[...].astype(F32)).astype(BF)


def sum_keys(own, received, earlier=()):
    rows, width = own[0].shape
    tile = rows // 4
    block = pl.BlockSpec((tile, width), lambda i: (i, 0))
    return run(
        "sum_keys",
        sum_keys_kernel,
        [*own, *received],
        [block] * 4,
        earlier,
        6,
        grid=(4,),
        out_specs=pl.BlockSpec((tile, 2 * width), lambda i: (i, 0)),
        out_shape=jax.ShapeDtypeStruct((rows, 2 * width), BF),
    )


def norm_scale(stream):
    return lax.rsqrt(jnp.mean(stream * stream, axis=-1, keepdims=True) + EPSILON)


def norm_back(stream, scale, gain, incoming):
    scaled = incoming * gain
    along = jnp.mean(scaled * stream, axis=-1, keepdims=True)
    return (
        scale * scaled - stream * (scale * scale * scale) * along,
        jnp.sum(incoming * stream * scale, axis=0, keepdims=True),
    )


def gate_and_slope(u):
    inner = 0.7978845608028654 * (u + 0.044715 * u * u * u)
    bent = jnp.tanh(inner)
    half = 0.5 * (1.0 + bent)
    slope = half + 0.5 * u * (1.0 - bent * bent) * 0.7978845608028654 * (1.0 + 0.134145 * u * u)
    return u * half, slope


def row_scale(stream):
    return lax.rsqrt(jnp.mean(stream * stream, axis=-1, keepdims=True) + EPSILON)


def norm_back_kernel(count, follows, *refs):
    stream_ref, gain_ref, upper_ref = refs[:3]
    if count:
        grad_refs, weight_ref, refs = refs[3 : 3 + count], refs[3 + count], refs[4 + count :]
        incoming, first = 0.0, 0
        for grad_ref in grad_refs:
            width = grad_ref.shape[1]
            incoming = incoming + nt(grad_ref[...], weight_ref[:, first : first + width])
            first += width
    else:
        incoming, refs = refs[3][...], refs[4:]
    next_ref, refs = (refs[0], refs[1:]) if follows else (None, refs)
    stream = stream_ref[...].astype(F32)
    scale = row_scale(stream)
    scaled = incoming * gain_ref[...]
    along = jnp.mean(scaled * stream, axis=-1, keepdims=True)
    grad = upper_ref[...].astype(F32) + (scale * scaled - stream * (scale * scale * scale) * along)

    @pl.when(pl.program_id(0) == 0)
    def _():
        refs[0][...] = jnp.zeros_like(refs[0])

    refs[0][...] += jnp.sum(incoming * stream * scale, axis=0, keepdims=True)
    low = grad.astype(BF)
    if follows:
        refs[1][...] = low
        refs[2][...] = grad
        refs[3][...] = nn(low, next_ref[...]).astype(BF)
    else:
        for i, ref in enumerate(refs[1:]):

            @pl.when(pl.program_id(0) == i)
            def _(ref=ref):
                ref[...] = low


def norm_back_call(stream, gain, upper, grads, weight, following=None, earlier=()):
    rows, model = stream.shape
    count, follows = (len(grads), following is not None) if weight is not None else (0, following is not None)
    tile = pl.BlockSpec((WIN, model), lambda i: (i, 0))

    def whole(x):
        return pl.BlockSpec(x.shape, lambda i: (0, 0))

    operands = [stream, gain, upper, *grads]
    specs = [tile, whole(gain), tile] + [
        pl.BlockSpec((WIN, x.shape[1]), lambda i: (i, 0)) for x in grads
    ]
    for x in (weight, following):
        if x is not None:
            operands.append(x)
            specs.append(whole(x))
    if follows:
        outs = [(rows, kind) for kind in (BF, F32, BF)]
        out_specs = [tile] * 3
    else:
        outs = [(WIN, BF)] * (rows // WIN)
        out_specs = [pl.BlockSpec((WIN, model), lambda i: (0, 0))] * (rows // WIN)
    return run(
        "norm_back",
        functools.partial(norm_back_kernel, count, follows),
        operands,
        specs,
        earlier,
        5,
        grid=(rows // WIN,),
        out_specs=[whole(gain)] + out_specs,
        out_shape=[jax.ShapeDtypeStruct(gain.shape, F32)]
        + [jax.ShapeDtypeStruct((n, model), kind) for n, kind in outs],
        compiler_params=pltpu.CompilerParams(vmem_limit_bytes=48 * MIB),
    )


def feed_forward_kernel(
    n_ref, g_ref, x_ref, in_ref, out_ref, act_ref, pre_ref, back_ref, low_ref, high_ref, sum_ref
):
    step = pl.program_id(0)
    half = n_ref.shape[0] // 2

    @pl.when(step == 0)
    def _():
        sum_ref[...] = x_ref[...]
        back_ref[...] = jnp.zeros_like(back_ref)

    for rows in (slice(0, half), slice(half, 2 * half)):
        gate, slope = gate_and_slope(nn(n_ref[rows, :], in_ref[...]))
        activated = gate.astype(BF)
        act_ref[rows, :] = activated
        sum_ref[rows, :] += nt(activated, out_ref[...])
        pre_grad = (nn(g_ref[rows, :], out_ref[...]) * slope).astype(BF)
        pre_ref[rows, :] = pre_grad
        back_ref[rows, :] += nt(pre_grad, in_ref[...])

    @pl.when(step == pl.num_programs(0) - 1)
    def _():
        low_ref[...] = sum_ref[:half].astype(BF)
        high_ref[...] = sum_ref[half:].astype(BF)


def feed_forward(rows, grads, stream, in_weight, out_weight, earlier=()):
    count, model = rows.shape
    units, tile = in_weight.shape[1], 512
    whole = pl.BlockSpec((count, model), lambda i: (0, 0))
    half = pl.BlockSpec((count // 2, model), lambda i: (0, 0))
    weight = pl.BlockSpec((model, tile), lambda i: (0, i))
    part = pl.BlockSpec((count, tile), lambda i: (0, i))
    return run(
        "feed_forward",
        feed_forward_kernel,
        [rows, grads, stream, in_weight, out_weight],
        [whole, whole, whole, weight, weight],
        earlier,
        16,
        grid=(units // tile,),
        out_specs=[part, part, whole, half, half],
        out_shape=[jax.ShapeDtypeStruct((count, units), BF)] * 2
        + [jax.ShapeDtypeStruct((count, model), F32)]
        + [jax.ShapeDtypeStruct((count // 2, model), BF)] * 2,
        scratch_shapes=[pltpu.VMEM((count, model), F32)],
        compiler_params=pltpu.CompilerParams(vmem_limit_bytes=48 * MIB),
    )


def local(
    hidden, passages, block_ids, buckets, norm_gains, self_query, self_key, self_value, self_out,
    cross_query, cross_key, cross_value, cross_out, ffn_in, ffn_out, rel_bias, out_grad,
):
    ranks = lax.axis_size("tensor")
    rank = lax.axis_index("tensor")
    batches, rows, model = hidden.shape
    head_width = self_query.shape[1]
    width = head_width * ranks

    hw, ffn = head_width, ffn_in.shape[1]
    self_layout = [(k * hw, hw, k * width, hw) for k in range(5)]
    kv_layout = [(0, hw, 0, hw), (hw, hw, width, hw)]
    late_layout = [(0, ffn, 0, ffn), (ffn, ffn, ranks * ffn, ffn), (2 * ffn, hw, 2 * ranks * ffn, hw)]
    def option(name, *choices):
        return choices[OPT[name] % len(choices)]

    gains = gather_small(jnp.transpose(norm_gains))
    gains = jnp.transpose(gains, (1, 0, 2)).reshape(3, model).astype(F32)
    if OPT["S"] == 0:
        self_blocks = gather_ranks([self_query, self_key, self_value, self_out, cross_query])
        kv_blocks = gather_ranks([cross_key, cross_value])
    else:
        both = beside([self_query, self_key, self_value, self_out, cross_query, cross_key, cross_value])
        both = lax.all_gather(both, "tensor", axis=0)
        cut = 5 * hw
        self_blocks, kv_blocks = [both[:, :, :cut]], [both[:, :, cut:]]
    if OPT["R"] == 0:
        ids = lax.dynamic_slice_in_dim(block_ids, rank * rows, rows, 1)
        stream_low, ids, _, _ = gathered_with_ids(hidden, ids)
    else:
        ids = gathered(
            lax.dynamic_slice_in_dim(block_ids, rank * rows, rows, 1).reshape(batches, -1, WIN)
        )
        stream_low = gathered(hidden)
    encoded = gathered(passages)
    bias = window_bias(
        rel_bias,
        buckets,
        option(
            "C",
            [gains, *self_blocks, *kv_blocks],
            [gains, *self_blocks],
            [gains, *kv_blocks],
            [gains, stream_low],
            [gains, encoded],
        ),
    )
    self_pieces = gather_cores(gather_far(gather_paths(jnp.stack(self_blocks) if OPT["S"] == 0 else self_blocks[0])))
    qkv_weight, so_weight, cq_weight = gather_end(
        self_pieces,
        [self_layout[:3], [(3 * hw, hw, 0, hw)], [(4 * hw, hw, 0, hw)]],
        option("B", [bias, stream_low], [bias], [bias, encoded], []),
        OPT["S"] == 0,
    )
    late_earlier = option(
        "A", self_blocks + kv_blocks, [bias], [stream_low], [encoded], [*kv_blocks, stream_low, bias],
        self_pieces[3:4], [qkv_weight], [*self_pieces[3:4], stream_low],
    )
    if OPT["Q"] == 0:
        late_blocks = gather_ranks_at_once([ffn_in, ffn_out, cross_out], late_earlier)
    else:
        late_blocks = jnp.stack(gather_ranks([ffn_in, ffn_out, cross_out], late_earlier))
    late_paths = gather_paths(late_blocks)
    kv_pieces = gather_cores(gather_far(gather_paths(jnp.stack(kv_blocks) if OPT["S"] == 0 else kv_blocks[0])))
    (kv_weight,) = gather_end(kv_pieces, [kv_layout], option("D", [qkv_weight], [bias], [encoded]), OPT["S"] == 0)

    stream = stream_low.astype(F32)
    scale_one = norm_scale(stream)
    normed_one = (stream * scale_one * gains[0]).astype(BF)
    qkv = nn(normed_one, qkv_weight).astype(BF)
    context = self_forward(qkv, ids, bias, [kv_weight])
    after_self = stream + nt(context, so_weight)
    scale_two = norm_scale(after_self)
    normed_two = (after_self * scale_two * gains[1]).astype(BF)
    queries = nn(normed_two, cq_weight).astype(BF)

    own_kv = nn(encoded, kv_weight).astype(BF)
    other_kv = flip(own_kv, "fsdp", 1)
    late_far = gather_far(late_paths)
    incoming = gathered_after(out_grad, option("T", [qkv_weight], [context], [own_kv], late_paths[:1], late_far[3:]))
    cross_context, exact, total = cross_forward(
        queries, own_kv, other_kv, option("E", late_paths[1:], [], late_far[3:], [incoming])
    )
    late_pieces = gather_cores(late_far)
    in_weight, out_weight, co_weight = gather_end(
        late_pieces,
        [[(0, ffn, 0, ffn)], [(ffn, ffn, 0, ffn)], [(2 * ffn, hw, 0, hw)]],
        [cross_context],
        OPT["Q"] != 0,
    )

    after_cross = after_self + nt(cross_context, co_weight)
    scale_three = norm_scale(after_cross)
    normed_three = (after_cross * scale_three * gains[2]).astype(BF)
    if OPT["F"] == 0:
        activated, pre_grad, normed_grad, *output = feed_forward(
            normed_three, incoming, after_cross, in_weight, out_weight
        )
    else:
        gate, slope = gate_and_slope(nn(normed_three, in_weight))
        activated = gate.astype(BF)
        output = (after_cross + nt(activated, out_weight)).astype(BF)
        output = [output[:WIN], output[WIN:]]
        pre_grad = (nn(incoming, out_weight) * slope).astype(BF)
        normed_grad = nt(pre_grad, in_weight)
    stream_part, gain_three = norm_back(after_cross, scale_three, gains[2], normed_grad)
    grad_two = incoming.astype(F32) + stream_part
    branch_two = grad_two.astype(BF)
    context_grad = nn(branch_two, co_weight).astype(BF)
    late_grads = weight_grads(
        [normed_three, incoming, branch_two],
        [((0,), [pre_grad]), ((1,), [activated]), ((2,), [cross_context])],
        [context_grad],
    )
    late_stage = scatter_cores(late_grads)

    query_grad, key_own, value_own, key_other, value_other = cross_backward(
        queries, context_grad, exact, total, own_kv, other_kv,
        option("G", [late_grads[0], output[0]], [late_grads[0]], [output[0]]),
    )
    output = returned(output)
    kv_received = [flip(x, "fsdp", 1) for x in (key_other, value_other)]
    late_stage = scatter_paths(late_stage, [query_grad])
    if OPT["H"] == 0:
        normed_grad = nt(query_grad, cq_weight)
        stream_part, gain_two = norm_back(after_self, scale_two, gains[1], normed_grad)
        grad_one = grad_two + stream_part
        branch_one = grad_one.astype(BF)
        context_grad = nn(branch_one, so_weight).astype(BF)
    else:
        gain_two, branch_one, grad_one, context_grad = norm_back_call(
            after_self, gains[1][None], grad_two, [query_grad], cq_weight, so_weight,
            option("H", [], [], [late_stage[0]]),
        )
    kv_grad = sum_keys([key_own, value_own], kv_received, [late_stage[0]])
    encoded_grad = rows_back(kv_grad, kv_weight)
    encoded_grads = returned(encoded_grad)

    gq, gk, gv, sums = self_backward(
        qkv, context_grad, ids, bias,
        option("I", [encoded_grad[0], *late_stage[1:]], [encoded_grad[0]], [late_stage[0]], []),
    )
    late_stage = scatter_far(late_stage, [gq])
    self_grads = weight_grads(
        [normed_one, branch_one, normed_two],
        [((0,), [gq]), ((0,), [gk]), ((0,), [gv]), ((1,), [context]), ((2,), [query_grad])],
        option("J", late_stage[:1], []),
    )
    self_stage = scatter_cores(self_grads)
    kv_sums = weight_grads([encoded], [((0,), [kv_grad])], [self_grads[0]])
    kv_stage = scatter_cores(kv_sums)
    if OPT["K"] == 0:
        late_blocks = scatter_end(late_stage, late_layout, [kv_sums[0]])
        self_stage = scatter_paths(self_stage, [late_blocks])
    else:
        self_stage = scatter_paths(self_stage, [kv_sums[0]])
        late_blocks = scatter_end(late_stage, late_layout, [self_stage[0]])
    kv_stage = scatter_paths(kv_stage, [self_stage[0], late_blocks])
    late_total = scatter_tensor(late_blocks)
    in_total, out_total, co_total = late_total[:, :ffn], late_total[:, ffn : 2 * ffn], late_total[:, 2 * ffn :]
    if OPT["L"] == 0:
        gain_one, *input_grad = norm_back_call(
            stream_low, gains[0][None], grad_one, [gq, gk, gv], qkv_weight, None, [self_stage[0]]
        )
    elif OPT["L"] == 1:
        gain_one, *input_grad = norm_back_call(
            stream_low, gains[0][None], grad_one, [gq, gk, gv], qkv_weight, None, [kv_stage[0]]
        )
    else:
        normed_grad = sum(
            nt(x, qkv_weight[:, k * width : (k + 1) * width]) for k, x in enumerate((gq, gk, gv))
        )
        stream_part, gain_one = norm_back(stream, scale_one, gains[0], normed_grad)
        input_grad = (grad_one + stream_part).astype(BF)
        input_grad = [input_grad[:WIN], input_grad[WIN:]]
    input_grads = returned(input_grad)
    bias_lanes = bucket_sums(
        sums, buckets, rel_bias.shape[0], option("M", [kv_stage[0]], [self_stage[0]], [self_stage[0], input_grad[0]])
    )
    self_stage = scatter_far(self_stage, option("N", [bias_lanes], [kv_stage[0]], [input_grad[0]]))
    kv_stage = scatter_far(kv_stage, [self_stage[0]])
    self_total = scatter_tensor(scatter_end(self_stage, self_layout, option("P", [kv_stage[0]], [])))
    q_total, k_total, v_total, so_total, cq_total = column_blocks(self_total, 5)
    kv_total = scatter_tensor(scatter_end(kv_stage, kv_layout, [kv_stage[0]]))

    bias_own = jnp.transpose(jnp.sum(bias_lanes, axis=2))
    small = jnp.concatenate(
        [gain_one.reshape(-1), gain_two.reshape(-1), gain_three.reshape(-1), bias_own.reshape(-1)]
    )
    pad = -small.shape[0] % 1024
    small = jnp.pad(small, (0, pad)).reshape(8, -1)
    small = sum_everywhere(small).reshape(-1)
    gains_sum = jnp.transpose(small[: 3 * model].reshape(3, model))
    bias_total = small[3 * model : 3 * model + rel_bias.size].reshape(rel_bias.shape)

    return (
        by_batch(output, BF),
        by_batch(input_grads, F32),
        by_batch(encoded_grads, F32),
        gains_sum,
        q_total,
        k_total,
        v_total,
        so_total,
        cq_total,
        kv_total[:, :head_width],
        kv_total[:, head_width:],
        co_total,
        in_total,
        out_total,
        bias_total,
    )


def solution(mesh):
    rows = P(None, ("fsdp", "tensor"), None)
    weight = P("fsdp", "tensor")
    in_specs = (rows, rows, P(None, "fsdp"), P(), P("fsdp", None)) + (weight,) * 10 + (P(), rows)
    out_specs = (rows, rows, rows, P()) + (weight,) * 10 + (P(),)
    return jax.shard_map(local, mesh=mesh, in_specs=in_specs, out_specs=out_specs, check_vma=False)
```
